256 devices in a mesh: row: 64 (over y, z, core), col: 4 (over x).
Axes of the slice: x: 4, y: 4, z: 8, core: 2. Of those that a mesh axis runs over, the one named last changes fastest.
Arguments:
- panel_matrix: float32 [65536, 512], P(('row', 'col')), may hold values from -1 to 1, as said below
- trailing: float32 [65536, 4096], P('row', 'col'), may hold values from -6 to 6
Outputs:
- r_factor: float32 [512, 512], replicated
- coupling: float32 [512, 4096], P(None, 'col')
- projected: float32 [65536, 4096], P('row', 'col')
The draws below stay inside these ranges and needn't reach their ends.
Inputs may be any that keep to these rules, and one draw needn't show every extreme that they name: panel_matrix has full column rank 512.
All inputs are finite; a program needn't handle non-finite values.
Results may differ from the reference program's by a relative error of at most 0.000088.
Values sent between devices are 32-bit elements; how exact they have to be, the bound alone decides.
A program may use at most 64 MiB of HBM per device.

```python
import math
import jax
import jax.numpy as jnp
from jax import lax

PANEL = 512
ROWS = 65536
TRAIL = 4096


def draw_panel_matrix(key, part):
    first_key, second_key = jax.random.split(jax.random.fold_in(key, 17))
    position = jnp.arange(ROWS, dtype=jnp.float32) / (ROWS - 1)
    spread = math.log(10.0)
    values = jnp.clip(jax.random.normal(first_key, (ROWS, PANEL), jnp.float32), -6.0, 6.0)
    rough = jnp.exp(jax.random.uniform(second_key, (ROWS, 1), jnp.float32, math.log(0.5), math.log(2.0)))
    scales = jnp.exp(spread * position)[:, None] * rough
    return values * scales / (4.0 * jnp.sqrt(10.0 * ROWS))


def block_levels(key, extent, cuts, least, largest):
    level = 1.0
    for dim, parts in cuts:
        draws = jax.random.uniform(jax.random.fold_in(jax.random.fold_in(key, 6), dim), (parts,), jnp.float32, least / len(cuts), largest / len(cuts))
        level = level * jnp.repeat(jnp.exp(draws), extent[dim] // parts).reshape((-1,) + (1,) * (len(extent) - 1 - dim))
    return level


def scatter_about(own_key, dims, deviation, bound, cuts=(), kind=jnp.bfloat16):
    entries = jax.random.normal(own_key, dims, jnp.float32) * deviation
    if len(cuts) > 0:
        entries = block_levels(own_key, dims, cuts, -0.22, 0.18) * entries
    return jnp.clip(entries, min=-bound, max=bound).astype(kind)


def setup_inputs(seed: int = 0) -> dict:
    keys = jax.random.split(jax.random.key(seed), 3)
    panel_matrix = draw_panel_matrix(jax.random.fold_in(keys[2], 71), 0)
    trailing = scatter_about(keys[1], (ROWS, TRAIL), 1.0, 6.0, ((0, 64), (1, 4)), jnp.float32)
    return dict(panel_matrix=panel_matrix, trailing=trailing)


def reference(panel_matrix, trailing):
    precise = lax.Precision.HIGHEST
    gram = jnp.dot(panel_matrix.T.astype(jnp.float32), panel_matrix.astype(jnp.float32), precision=precise, preferred_element_type=jnp.float32)
    lower_factor = jnp.linalg.cholesky(gram)
    basis = jax.scipy.linalg.solve_triangular(lower_factor, panel_matrix.T, lower=True).T
    coupling = jnp.dot(basis.T.astype(jnp.float32), trailing.astype(jnp.float32), precision=precise, preferred_element_type=jnp.float32)
    projected = trailing - jnp.dot(basis.astype(jnp.float32), coupling.astype(jnp.float32), precision=precise, preferred_element_type=jnp.float32)
    return (lower_factor.T, coupling, projected)
```

```python
import jax
import jax.numpy as jnp
from jax import lax
from jax.experimental import pallas as pl
from jax.experimental.pallas import tpu as pltpu
from jax.sharding import PartitionSpec as P

HI = lax.Precision.HIGHEST
F32 = jnp.float32
BF16 = jnp.bfloat16
MESH = pl.DeviceIdType.MESH

NX, NY, NZ = 4, 4, 8
BLOCKS = [(i, j) for i in range(4) for j in range(i, 4)]
WP, WQ = 768, 256


def split(x):
    hi = x.astype(BF16)
    return hi, (x - hi.astype(F32)).astype(BF16)


def dot(a, b):
    return jnp.dot(a, b, preferred_element_type=F32)


def dot3(ah, al, bh, bl):
    return dot(ah, bh) + (dot(ah, bl) + dot(al, bh))


def dot_hi(a, b):
    return jnp.dot(a, b, precision=HI, preferred_element_type=F32)


def factor128(S, X):
    n = len(S)
    sub = lax.broadcasted_iota(jnp.int32, (8, 128), 0)
    S, X = list(S), list(X)
    for g in range(n):
        C = {}
        for h in range(g, n):
            for c in range(8):
                C[c, h] = jnp.broadcast_to(S[h][:, 8 * g + c : 8 * g + c + 1], (8, 128))
        D = jnp.zeros((8, 128), F32)
        for k in range(8):
            piv = jnp.broadcast_to(C[k, g][k : k + 1, :], (8, 128))
            rinv = 1.0 / piv
            D = jnp.where(sub == k, piv, D)
            row_s = jnp.broadcast_to(S[g][k : k + 1, :], (8, 128))
            row_x = jnp.broadcast_to(X[g][k : k + 1, :], (8, 128))
            row_c = {c: jnp.broadcast_to(C[c, g][k : k + 1, :], (8, 128)) for c in range(k + 1, 8)}
            for h in range(g, n):
                m = C[k, h]
                if h == g:
                    if k == 7:
                        continue
                    m = jnp.where(sub > k, m, 0.0)
                for c in range(k + 1, 8):
                    C[c, h] = C[c, h] - (m * row_c[c]) * rinv
                t = m * rinv
                S[h] = S[h] - t * row_s
                X[h] = X[h] - t * row_x
        scale = lax.rsqrt(D)
        S[g] = S[g] * scale
        X[g] = X[g] * scale
    return S, X


def chol_block(J, s_ref, r_ref, x_ref):
    o = pl.multiple_of(J * 128, 128)
    sub = lax.broadcasted_iota(jnp.int32, (8, 128), 0)
    lan = lax.broadcasted_iota(jnp.int32, (8, 128), 1)
    S = [s_ref[pl.ds(pl.multiple_of(o + 8 * g, 8), 8), pl.ds(o, 128)] for g in range(16)]
    X = [jnp.where(sub + 8 * g == lan, 1.0, 0.0).astype(F32) for g in range(16)]
    R, L = factor128(S, X)
    for g in range(16):
        rows = pl.ds(pl.multiple_of(o + 8 * g, 8), 8)
        r_ref[rows, pl.ds(o, 128)] = jnp.where(lan >= sub + 8 * g, R[g], 0.0)
        x_ref[rows, pl.ds(o, 128)] = L[g]


def chol_update(j, s_ref, r_ref, x_ref):
    a, b = j * 128, j * 128 + 128
    li = x_ref[a:b, a:b]
    if j > 0:
        x_ref[a:b, :a] = dot_hi(li, x_ref[a:b, :a])
    if j < 3:
        r12 = dot_hi(li, s_ref[a:b, b:])
        r_ref[a:b, b:] = r12
        r12t = r12.T
        for i in range(j + 1, 4):
            p, q = i * 128, i * 128 + 128
            left = r12t[p - b : q - b, :]
            s_ref[p:q, p:] = s_ref[p:q, p:] - dot_hi(left, r12[:, p - b :])
            x_ref[p:q, :b] = x_ref[p:q, :b] - dot_hi(left, x_ref[a:b, :b])


def comm_kernel(
    a_ref, t_ref,
    r_ref, x_ref, ag, wo_p, wo_q,
    s_ref, gb, gcl, ga, gl1p, gr1p, gl2p, gl1q, gr1q, gl2q, xb, go,
    wp_p, wp_q, wc_p, wc_q, wl1p, wr1p, wl2p, wl1q, wr1q, wl2q,
    send, recv, lsem,
):
    r = lax.axis_index("row")
    x = lax.axis_index("col")
    c = r % 2
    z = (r // 2) % NZ
    y = r // (2 * NZ)

    def at_y(d):
        return {"row": (((y + d) % NY) * NZ + z) * 2 + c}

    def at_z(d):
        return {"row": (y * NZ + (z + d) % NZ) * 2 + c}

    def at_x(d):
        return {"col": (x + d) % NX}

    sibling = {"row": r + 1 - 2 * c}
    axes = {"y": (NY, y, at_y), "z": (NZ, z, at_z)}

    counter = [0]

    def group(n):
        base = counter[0]
        counter[0] += n
        return base

    pending = []

    def copy(k, src, dst, to):
        return pltpu.make_async_remote_copy(
            src_ref=src, dst_ref=dst, send_sem=send.at[k], recv_sem=recv.at[k], device_id=to, device_id_type=MESH
        )

    def scatter(axis, buf, land, piece):
        n, i, at = axes[axis]
        base = group(n - 1)
        return [
            (lambda d=d: copy(base + d - 1, buf.at[pl.ds(((i + d) % n) * piece, piece)], land.at[d - 1], at(d)))
            for d in range(1, n)
        ]

    def gather(axis, buf, piece, start):
        n, i, at = axes[axis]
        base = group(n - 1)
        rows = pl.ds(start + i * piece, piece)
        return [(lambda d=d: copy(base + d - 1, buf.at[rows], buf.at[rows], at(d))) for d in range(1, n)]

    def single(src, dst, to):
        base = group(1)
        return [lambda: copy(base, src, dst, to)]

    def start(copies):
        for f in copies:
            f().start()
        pending.extend(copies)

    def arrive(copies):
        for f in copies:
            f().wait_recv()

    def reduce_into(axis, buf, land, piece):
        n, i, _ = axes[axis]
        total = buf[pl.ds(pl.multiple_of(i * piece, 8), piece), :]
        for d in range(n - 1):
            total = total + land[d]
        return total

    barrier = pltpu.get_barrier_semaphore()
    peers = [sibling] + [at_y(d) for d in range(1, NY)] + [at_z(d) for d in range(1, NZ)] + [at_x(d) for d in range(1, NX)]
    for p in peers:
        pl.semaphore_signal(barrier, inc=1, device_id=p, device_id_type=MESH)
    pl.semaphore_wait(barrier, len(peers))

    left, right = (x + NX - 1) % NX, (x + 1) % NX
    a_right = single(a_ref, ag.at[x], at_x(1))
    a_left = single(a_ref, ag.at[x], at_x(NX - 1))
    start(a_right)
    start(a_left)
    ag[x] = a_ref[...]

    a_own = a_ref[...]
    a_own_t = a_own.T
    for i in range(4):
        rows = dot_hi(a_own_t[i * 128 : i * 128 + 128], a_own[:, i * 128 :])
        for j in range(i, 4):
            n = BLOCKS.index((i, j))
            gb[n // 5, (n % 5) * 128 : (n % 5) * 128 + 128, :] = rows[:, (j - i) * 128 : (j - i) * 128 + 128]
    g_core = single(gb.at[1 - c], gcl, sibling)
    start(g_core)

    def w_block(b, first):
        ah, al = split(ag[b].T)

        def chunk(out, rows, cols):
            th, tl = split(t_ref[rows, cols])
            return dot3(ah, al, th, tl)

        rows = pl.ds(pl.multiple_of(b * 256, 256), 256)

        def add(ref, cols_out, v):
            for half in range(2):
                part = v[half * 256 : half * 256 + 256]
                if first:
                    ref[half, :, cols_out] = part
                else:
                    ref[half, :, cols_out] = ref[half, :, cols_out] + part

        def body(n, carry):
            cols = pl.ds(pl.multiple_of(n * 256, 256), 256)
            add(wp_p, cols, chunk(wp_p, rows, cols))
            return carry

        lax.fori_loop(0, WP // 256, body, 0)
        add(wp_q, pl.ds(0, WQ), chunk(wp_q, rows, pl.ds(WP, WQ)))

    w_block(x, True)

    arrive(g_core)
    ga[0:640] = gb[c, 0:640] + gcl[...]
    ga[640:768] = jnp.zeros((128, 128), F32)
    g1p = scatter("y", ga.at[0:512], gl1p, 128)
    g1q = scatter("z", ga.at[512:768], gl1q, 32)
    start(g1p)
    start(g1q)
    arrive(g1p)
    arrive(g1q)
    gr1p[...] = reduce_into("y", ga.at[0:512], gl1p, 128)
    gr1q[...] = reduce_into("z", ga.at[512:768], gl1q, 32)
    g2p = scatter("z", gr1p, gl2p, 16)
    g2q = scatter("y", gr1q, gl2q, 8)
    start(g2p)
    start(g2q)

    arrive(a_right)
    arrive(a_left)
    on_right = single(ag.at[left, 0:128], ag.at[left, 0:128], at_x(1))
    on_left = single(ag.at[right, 128:256], ag.at[right, 128:256], at_x(NX - 1))
    start(on_right)
    start(on_left)

    arrive(g2p)
    arrive(g2q)
    xb[x, 0:16] = reduce_into("z", gr1p, gl2p, 16)
    xb[x, 16:24] = reduce_into("y", gr1q, gl2q, 8)
    base = group(NX - 1)
    g_x = [(lambda d=d: copy(base + d - 1, xb.at[x], xb.at[x], at_x(d))) for d in range(1, NX)]
    start(g_x)
    w_block(left, False)
    arrive(g_x)
    total = (xb[0] + xb[1]) + (xb[2] + xb[3])
    go[c, pl.ds(pl.multiple_of(y * 128 + z * 16, 8), 16), :] = total[0:16]
    go[c, pl.ds(pl.multiple_of(512 + z * 32 + y * 8, 8), 8), :] = total[16:24]
    g3p = gather("z", go.at[c], 16, y * 128)
    g3q = gather("y", go.at[c], 8, 512 + z * 32)
    start(g3p)
    start(g3q)
    w_block(right, False)
    arrive(g3p)
    arrive(g3q)
    g4p = gather("y", go.at[c], 128, 0)
    g4q = gather("z", go.at[c], 32, 512)
    start(g4p)
    start(g4q)
    arrive(on_right)
    arrive(on_left)
    w_block((x + 2) % NX, False)
    w_core_p = single(wp_p.at[1 - c], wc_p, sibling)
    w_core_q = single(wp_q.at[1 - c], wc_q, sibling)
    start(w_core_p)
    start(w_core_q)
    arrive(g4p)
    arrive(g4q)
    g_core2 = single(go.at[c, 0:640], go.at[c, 0:640], sibling)
    start(g_core2)
    arrive(g_core2)
    for n, (i, j) in enumerate(BLOCKS):
        s_ref[i * 128 : i * 128 + 128, j * 128 : j * 128 + 128] = go[n // 5, (n % 5) * 128 : (n % 5) * 128 + 128, :]

    x_ref[...] = jnp.zeros_like(x_ref)
    r_ref[...] = jnp.zeros_like(r_ref)

    w1p = scatter("y", wp_p.at[c], wl1p, 64)
    w1q = scatter("z", wp_q.at[c], wl1q, 32)
    w2p = scatter("z", wr1p, wl2p, 8)
    w2q = scatter("y", wr1q, wl2q, 8)
    w3p = gather("z", wo_p.at[c], 8, y * 64)
    w3q = gather("y", wo_q.at[c], 8, z * 32)
    w4p = gather("y", wo_p.at[c], 64, 0)
    w4q = gather("z", wo_q.at[c], 32, 0)
    w5p = single(wo_p.at[c], wo_p.at[c], sibling)
    w5q = single(wo_q.at[c], wo_q.at[c], sibling)

    def w_step(j):
        if j == 0:
            arrive(w_core_p)
            arrive(w_core_q)
            wp_p[c] = wp_p[c] + wc_p[...]
            wp_q[c] = wp_q[c] + wc_q[...]
            start(w1p)
            start(w1q)
        if j == 1:
            arrive(w1p)
            arrive(w1q)
            wr1p[...] = reduce_into("y", wp_p.at[c], wl1p, 64)
            wr1q[...] = reduce_into("z", wp_q.at[c], wl1q, 32)
            start(w2p)
            start(w2q)
        if j == 2:
            arrive(w2p)
            arrive(w2q)
            wo_p[c, pl.ds(pl.multiple_of(y * 64 + z * 8, 8), 8), :] = reduce_into("z", wr1p, wl2p, 8)
            wo_q[c, pl.ds(pl.multiple_of(z * 32 + y * 8, 8), 8), :] = reduce_into("y", wr1q, wl2q, 8)
            start(w3p)
            start(w3q)
        if j == 3:
            arrive(w3p)
            arrive(w3q)
            start(w4p)
            start(w4q)

    def step(J, carry):
        for j in range(4):

            @pl.when(J == j)
            def _():
                w_step(j)

        chol_block(J, s_ref, r_ref, x_ref)
        for j in range(4):

            @pl.when(J == j)
            def _():
                chol_update(j, s_ref, r_ref, x_ref)

        return carry

    lax.fori_loop(0, 4, step, 0)

    arrive(w4p)
    arrive(w4q)
    start(w5p)
    start(w5q)
    arrive(w5p)
    arrive(w5q)
    for f in pending:
        f().wait_send()


def tail_kernel(t_ref, a_ref, x_ref, wp_ref, wq_ref, coupling_ref, out_ref, yh, yl):
    @pl.when(pl.program_id(0) == 0)
    def _():
        x = x_ref[...]
        xh, xl = split(x)
        xth, xtl = split(x.T)
        for n in range(4):
            if n < 3:
                w = jnp.concatenate([wp_ref[0, :, n * 256 : n * 256 + 256], wp_ref[1, :, n * 256 : n * 256 + 256]], 0)
            else:
                w = jnp.concatenate([wq_ref[0], wq_ref[1]], 0)
            wh, wl = split(w)
            cpl = dot3(xh, xl, wh, wl)
            coupling_ref[:, n * 256 : n * 256 + 256] = cpl
            ch, cl = split(cpl)
            yy = dot3(xth, xtl, ch, cl)
            h, l = split(yy)
            yh[:, n * 256 : n * 256 + 256] = h
            yl[:, n * 256 : n * 256 + 256] = l

    ah, al = split(a_ref[...])
    for n in range(4):
        cols = slice(n * 256, n * 256 + 256)
        out_ref[:, cols] = t_ref[:, cols] - dot3(ah, al, yh[:, cols], yl[:, cols])


def shards(panel_matrix, trailing):
    V = pl.BlockSpec(memory_space=pltpu.VMEM)
    f = lambda *s: jax.ShapeDtypeStruct(s, F32)
    v = lambda *s: pltpu.VMEM(s, F32)
    r, linv, ag, wo_p, wo_q = pl.pallas_call(
        comm_kernel,
        out_shape=(f(512, 512), f(512, 512), f(4, 256, 512), f(2, 256, WP), f(2, 256, WQ)),
        in_specs=[V, V],
        out_specs=(V,) * 5,
        scratch_shapes=[
            v(512, 512), v(2, 640, 128), v(640, 128), v(768, 128),
            v(3, 128, 128), v(128, 128), v(7, 16, 128),
            v(7, 32, 128), v(32, 128), v(3, 8, 128),
            v(4, 24, 128), v(2, 768, 128),
            v(2, 256, WP), v(2, 256, WQ), v(256, WP), v(256, WQ),
            v(3, 64, WP), v(64, WP), v(7, 8, WP),
            v(7, 32, WQ), v(32, WQ), v(3, 8, WQ),
            pltpu.SemaphoreType.DMA((110,)), pltpu.SemaphoreType.DMA((110,)), pltpu.SemaphoreType.DMA((2,)),
        ],
        name="reduce_and_factor",
        compiler_params=pltpu.CompilerParams(collective_id=0, has_side_effects=True, vmem_limit_bytes=48 * 2**20),
    )(panel_matrix, trailing)

    whole = lambda *s: pl.BlockSpec(s, lambda i: (0,) * len(s))
    coupling, projected = pl.pallas_call(
        tail_kernel,
        grid=(4,),
        out_shape=(f(512, 1024), f(1024, 1024)),
        in_specs=[
            pl.BlockSpec((256, 1024), lambda i: (i, 0)),
            pl.BlockSpec((None, 256, 512), lambda i: (i, 0, 0)),
            whole(512, 512),
            whole(2, 256, WP),
            whole(2, 256, WQ),
        ],
        out_specs=(whole(512, 1024), pl.BlockSpec((256, 1024), lambda i: (i, 0))),
        scratch_shapes=[pltpu.VMEM((512, 1024), BF16), pltpu.VMEM((512, 1024), BF16)],
        name="project",
        compiler_params=pltpu.CompilerParams(vmem_limit_bytes=48 * 2**20),
    )(trailing, ag, linv, wo_p, wo_q)
    return r, coupling, projected


def solution(mesh):
    in_specs = (P(("row", "col"), None), P("row", "col"))
    out_specs = (P(), P(None, "col"), P("row", "col"))
    return jax.shard_map(shards, mesh=mesh, in_specs=in_specs, out_specs=out_specs, check_vma=False)
```

```python
import jax
import jax.numpy as jnp
from jax import lax
from jax.experimental import pallas as pl
from jax.experimental.pallas import tpu as pltpu
from jax.sharding import PartitionSpec as P

HI = lax.Precision.HIGHEST
F32 = jnp.float32
BF16 = jnp.bfloat16
MESH = pl.DeviceIdType.MESH
B8 = (8, 128)

NX, NY, NZ = 4, 4, 8
BLOCKS0 = [(0, 0), (0, 1), (0, 2), (0, 3)]
BLOCKS1 = [(1, 1), (1, 2), (1, 3), (2, 2), (2, 3), (3, 3)]
WP = 768


def split(x):
    hi = x.astype(BF16)
    return hi, (x - hi.astype(F32)).astype(BF16)


def dot(a, b):
    return jnp.dot(a, b, preferred_element_type=F32)


def dot3(ah, al, bh, bl):
    return dot(ah, bh) + (dot(ah, bl) + dot(al, bh))


def dot_hi(a, b):
    return jnp.dot(a, b, precision=HI, preferred_element_type=F32)


def bc(v):
    return jnp.broadcast_to(v, B8)


def factor128(block):
    n, nb = 16, 8
    sub = lax.broadcasted_iota(jnp.int32, B8, 0)
    lan = lax.broadcasted_iota(jnp.int32, B8, 1)
    S = [block[8 * g : 8 * g + 8] for g in range(n)]
    X = [jnp.where(sub + 8 * g == lan, 1.0, 0.0).astype(F32) for g in range(n)]
    for b in range(0, n, nb):
        e = b + nb
        own = None
        for g in range(b, e):
            if own is None:
                own = [bc(S[g][:, 8 * g + c : 8 * g + c + 1]) for c in range(8)]
            C = {(c, g): own[c] for c in range(8)}
            N = None
            if g + 1 < e:
                N = [bc(S[g + 1][:, 8 * (g + 1) + c : 8 * (g + 1) + c + 1]) for c in range(8)]
            for h in range(g + 1, e):
                for c in range(8):
                    C[c, h] = bc(S[h][:, 8 * g + c : 8 * g + c + 1])
            D = jnp.zeros(B8, F32)
            for k in range(8):
                piv = bc(C[k, g][k : k + 1, :])
                rinv = 1.0 / piv
                D = jnp.where(sub == k, piv, D)
                row_s, row_x = bc(S[g][k : k + 1, :]), bc(X[g][k : k + 1, :])
                row_c = {c: bc(C[c, g][k : k + 1, :]) for c in range(k + 1, 8)}
                for h in range(g, e):
                    m = C[k, h]
                    if h == g:
                        if k == 7:
                            continue
                        m = jnp.where(sub > k, m, 0.0)
                        for c in range(k + 1, 8):
                            C[c, h] = C[c, h] - (m * row_c[c]) * rinv
                        t = m * rinv
                    else:
                        t = m * rinv
                        for c in range(k + 1, 8):
                            C[c, h] = C[c, h] - t * row_c[c]
                        if h == g + 1:
                            for c in range(8):
                                N[c] = N[c] - t * bc(m[c : c + 1, :])
                    S[h] = S[h] - t * row_s
                    X[h] = X[h] - t * row_x
            own = N
            scale = lax.rsqrt(D)
            S[g] = S[g] * scale
            X[g] = X[g] * scale
        if e < n:
            U = jnp.concatenate(S[b:e], 0)
            both = jnp.concatenate([U, jnp.concatenate(X[b:e], 0)], 1)
            up = dot_hi(U.T[8 * e :], both)
            for h in range(e, n):
                S[h] = S[h] - up[8 * (h - e) : 8 * (h - e) + 8, :128]
                X[h] = X[h] - up[8 * (h - e) : 8 * (h - e) + 8, 128:]
    R = [jnp.where(lan >= sub + 8 * g, S[g], 0.0) for g in range(n)]
    return jnp.concatenate(R, 0), jnp.concatenate(X, 0)


def comm_kernel(
    a_hbm, t_hbm,
    r_ref, p_ref, qh_ref, ql_ref, cpl_ref,
    ag, t_ref, th, tl, s_ref, x_ref, gb0, gb1, gc0, gc1, ga0, ga1,
    gl10, gr10, gl20, gl11, gr11, gl21, xb0, xb1, go0, go1,
    w_ref, wc, wo, wl1p, wr1p, wl2p, wl1q, wr1q, wl2q,
    send, recv, lsem,
):
    r = lax.axis_index("row")
    x = lax.axis_index("col")
    c = r % 2
    z = (r // 2) % NZ
    y = r // (2 * NZ)

    def at_y(d):
        return {"row": (((y + d) % NY) * NZ + z) * 2 + c}

    def at_z(d):
        return {"row": (y * NZ + (z + d) % NZ) * 2 + c}

    def at_x(d):
        return {"col": (x + d) % NX}

    sibling = {"row": r + 1 - 2 * c}
    axes = {"x": (NX, x, at_x), "y": (NY, y, at_y), "z": (NZ, z, at_z)}
    counter = [0]
    pending = []

    def copies(pairs):
        base = counter[0]
        counter[0] += len(pairs)

        def make(k, src, dst, to):
            return lambda: pltpu.make_async_remote_copy(
                src_ref=src, dst_ref=dst, send_sem=send.at[k], recv_sem=recv.at[k], device_id=to, device_id_type=MESH
            )

        return [make(base + k, *p) for k, p in enumerate(pairs)]

    def start(group):
        for f in group:
            f().start()
        pending.extend(group)

    def arrive(group):
        for f in group:
            f().wait_recv()

    def rows_of(n):
        return lambda i: (pl.ds(pl.multiple_of(i * n, 8), n), slice(None))

    def halves_of(cols):
        return lambda i: (pl.ds(pl.multiple_of(i // 2 * 8, 8), 8), pl.ds(pl.multiple_of(i % 2 * cols, 128), cols))

    def scatter(axis, ref, piece, land):
        n, i, at = axes[axis]
        return copies([(ref.at[piece((i + d) % n)], land.at[d - 1], at(d)) for d in range(1, n)])

    def summed(axis, ref, piece, land):
        n, i, _ = axes[axis]
        total = ref[piece(i)]
        for d in range(n - 1):
            total = total + land[d]
        return total

    def gather(axis, ref, piece):
        n, i, at = axes[axis]
        return copies([(ref.at[piece(i)], ref.at[piece(i)], at(d)) for d in range(1, n)])

    barrier = pltpu.get_barrier_semaphore()
    peers = [sibling] + [at_y(d) for d in range(1, NY)] + [at_z(d) for d in range(1, NZ)] + [at_x(d) for d in range(1, NX)]
    for p in peers:
        pl.semaphore_signal(barrier, inc=1, device_id=p, device_id_type=MESH)
    load_a = pltpu.make_async_copy(a_hbm, ag.at[x], lsem.at[0])
    load_t = pltpu.make_async_copy(t_hbm, t_ref, lsem.at[1])
    load_a.start()
    load_t.start()
    load_a.wait()

    a_own = ag[x]
    a_own_t = a_own.T
    for i in range(4):
        rows = dot_hi(a_own_t[i * 128 : i * 128 + 128], a_own[:, i * 128 :])
        for j in range(i, 4):
            part = rows[:, (j - i) * 128 : (j - i) * 128 + 128]
            if i == 0:
                n = BLOCKS0.index((i, j))
                gb0[n // 2, n % 2 * 128 : n % 2 * 128 + 128, :] = part
            else:
                n = BLOCKS1.index((i, j))
                gb1[n // 3, n % 3 * 128 : n % 3 * 128 + 128, :] = part

    pl.semaphore_wait(barrier, len(peers))

    g0_c = copies([(gb0.at[1 - c], gc0, sibling)])
    g1_c = copies([(gb1.at[1 - c], gc1, sibling)])
    start(g0_c)
    start(g1_c)
    left, right, opposite = (x + NX - 1) % NX, (x + 1) % NX, (x + 2) % NX
    half = [slice(0, 256), slice(256, 512)]
    a1 = [
        copies([(ag.at[x, :, half[k]], ag.at[x, :, half[k]], at_x(1)), (ag.at[x, :, half[k]], ag.at[x, :, half[k]], at_x(NX - 1))])
        for k in range(2)
    ]
    a2 = [
        copies([
            (ag.at[left, 0:128, half[k]], ag.at[left, 0:128, half[k]], at_x(1)),
            (ag.at[right, 128:256, half[k]], ag.at[right, 128:256, half[k]], at_x(NX - 1)),
        ])
        for k in range(2)
    ]
    start(a1[0])
    start(a1[1])

    def w_block(b, k, first=False):
        ah, al = split(ag[b, :, half[k]].T)
        rows = pl.ds(pl.multiple_of(b * 256, 256), 256)
        for n in range(4):
            cols = slice(n * 256, n * 256 + 256)
            v = dot3(ah, al, th[rows, cols], tl[rows, cols])
            for m in range(2):
                part = v[m * 128 : m * 128 + 128]
                w_ref[k, m, :, cols] = part if first else w_ref[k, m, :, cols] + part

    s10 = scatter("y", ga0, rows_of(64), gl10)
    s20 = scatter("z", gr10, rows_of(8), gl20)
    s11 = scatter("z", ga1, rows_of(64), gl11)
    s21 = scatter("y", gr11, rows_of(16), gl21)
    x0 = copies([(xb0.at[x], xb0.at[x], at_x(d)) for d in range(1, NX)])
    x1 = copies([(xb1.at[x], xb1.at[x], at_x(d)) for d in range(1, NX)])
    o20 = gather("z", go0.at[c], lambda i: (pl.ds(pl.multiple_of(y * 64 + i * 8, 8), 8), slice(None)))
    o10 = gather("y", go0.at[c], rows_of(64))
    o21 = gather("y", go1.at[c], lambda i: (pl.ds(pl.multiple_of(z * 64 + i * 16, 8), 16), slice(None)))
    o11 = gather("z", go1.at[c], rows_of(64))
    o_c0 = copies([(go0.at[c], go0.at[c], sibling)])
    o_c1 = copies([(go1.at[c, 0:384], go1.at[c, 0:384], sibling)])

    zp, zq = halves_of(384), halves_of(128)
    wk = [w_ref.at[k, c] for k in range(2)]
    ok = [wo.at[k, c] for k in range(2)]
    wp, wq = [f.at[:, 0:WP] for f in wk], [f.at[:, WP:1024] for f in wk]
    op, oq = [f.at[:, 0:WP] for f in ok], [f.at[:, WP:1024] for f in ok]
    w_c = [copies([(w_ref.at[k, 1 - c], wc.at[k], sibling)]) for k in range(2)]
    w1 = [scatter("y", wp[k], rows_of(32), wl1p.at[k]) + scatter("z", wq[k], rows_of(16), wl1q.at[k]) for k in range(2)]
    w2 = [scatter("z", wr1p.at[k], zp, wl2p.at[k]) + scatter("y", wr1q.at[k], zq, wl2q.at[k]) for k in range(2)]

    def piece_p(i):
        return (pl.ds(pl.multiple_of(y * 32 + i // 2 * 8, 8), 8), pl.ds(pl.multiple_of(i % 2 * 384, 128), 384))

    def piece_q(i):
        return (pl.ds(pl.multiple_of(z * 16 + i // 2 * 8, 8), 8), pl.ds(pl.multiple_of(i % 2 * 128, 128), 128))

    w3 = [gather("z", op[k], piece_p) + gather("y", oq[k], piece_q) for k in range(2)]
    w4 = [gather("y", op[k], rows_of(32)) + gather("z", oq[k], rows_of(16)) for k in range(2)]
    w5 = [copies([(ok[k], ok[k], sibling)]) for k in range(2)]

    def w_core(k):
        arrive(w_c[k])
        w_ref[k, c] = w_ref[k, c] + wc[k]
        start(w1[k])

    def w_first(k):
        arrive(w1[k])
        wr1p[k] = summed("y", wp[k], rows_of(32), wl1p.at[k])
        wr1q[k] = summed("z", wq[k], rows_of(16), wl1q.at[k])
        start(w2[k])

    def w_second(k):
        arrive(w2[k])
        op[k][piece_p(z)] = summed("z", wr1p.at[k], zp, wl2p.at[k])
        oq[k][piece_q(y)] = summed("y", wr1q.at[k], zq, wl2q.at[k])
        start(w3[k])

    def w_third(k):
        arrive(w3[k])
        start(w4[k])

    def w_last(k):
        arrive(w4[k])
        start(w5[k])

    arrive(g0_c)
    ga0[...] = gb0[c] + gc0[...]
    start(s10)
    arrive(g1_c)
    ga1[0:384] = gb1[c] + gc1[...]
    ga1[384:512] = jnp.zeros((128, 128), F32)
    start(s11)

    load_t.wait()
    th[...], tl[...] = split(t_ref[...])
    w_block(x, 0, True)

    arrive(s10)
    gr10[...] = summed("y", ga0, rows_of(64), gl10)
    start(s20)
    arrive(s11)
    gr11[...] = summed("z", ga1, rows_of(64), gl11)
    start(s21)
    arrive(a1[0])
    start(a2[0])
    w_block(left, 0)
    arrive(s20)
    xb0[x] = summed("z", gr10, rows_of(8), gl20)
    start(x0)
    arrive(s21)
    xb1[x] = summed("y", gr11, rows_of(16), gl21)
    start(x1)
    w_block(right, 0)
    arrive(a1[1])
    start(a2[1])
    arrive(x0)
    go0[c, pl.ds(pl.multiple_of(y * 64 + z * 8, 8), 8), :] = (xb0[0] + xb0[1]) + (xb0[2] + xb0[3])
    start(o20)
    arrive(x1)
    go1[c, pl.ds(pl.multiple_of(z * 64 + y * 16, 8), 16), :] = (xb1[0] + xb1[1]) + (xb1[2] + xb1[3])
    start(o21)
    arrive(a2[0])
    w_block(opposite, 0)
    start(w_c[0])
    w_block(x, 1, True)
    arrive(o20)
    start(o10)
    arrive(o21)
    start(o11)
    w_core(0)
    w_block(left, 1)
    w_block(right, 1)
    arrive(o10)
    start(o_c0)
    arrive(a2[1])
    w_block(opposite, 1)
    start(w_c[1])
    arrive(o_c0)
    for n, (i, j) in enumerate(BLOCKS0):
        s_ref[:128, j * 128 : j * 128 + 128] = go0[n // 2, n % 2 * 128 : n % 2 * 128 + 128, :]
    r_ref[...] = jnp.zeros_like(r_ref)
    x_ref[...] = jnp.zeros_like(x_ref)
    arrive(o11)
    start(o_c1)
    w_core(1)

    diag = s_ref[0:128, 0:128]
    for J in range(4):
        a, b, q = J * 128, J * 128 + 128, J * 128 + 256
        r11, li = factor128(diag)
        r_ref[a:b, a:b] = r11
        x_ref[a:b, a:b] = li
        if J == 0:
            arrive(o_c1)
            for n, (i, j) in enumerate(BLOCKS1):
                s_ref[i * 128 : i * 128 + 128, j * 128 : j * 128 + 128] = go1[n // 3, n % 3 * 128 : n % 3 * 128 + 128, :]
            w_first(0)
        if J == 1:
            w_first(1)
            w_second(0)
        if J == 2:
            w_third(0)
            w_second(1)
        if J < 3:
            r12 = dot_hi(li, s_ref[a:b, b:q])
            r_ref[a:b, b:q] = r12
            diag = s_ref[b:q, b:q] - dot_hi(r12.T, r12)
            if J < 2:
                r13 = dot_hi(li, s_ref[a:b, q:])
                r_ref[a:b, q:] = r13
                s_ref[b:q, q:] = s_ref[b:q, q:] - dot_hi(r12.T, r13)
                s_ref[q:, q:] = s_ref[q:, q:] - dot_hi(r13.T, r13)
        if J > 0:
            x_ref[a:b, :a] = dot_hi(li, x_ref[a:b, :a])
        if J < 3:
            x_ref[b:, :b] = x_ref[b:, :b] - dot_hi(r_ref[a:b, b:].T, x_ref[a:b, :b])
    w_third(1)

    xi = x_ref[...]
    xh, xl = split(xi)
    xth, xtl = split(xi.T)

    def basis(rows, cols):
        ah, al = split(ag[rows][:, : cols.stop])
        return split(dot3(ah, al, xth[: cols.stop, cols], xtl[: cols.stop, cols]))

    qa = [basis(b, half[0]) for b in range(4)]
    for b in range(4):
        qh_ref[b], ql_ref[b] = basis(b, half[1])
    w_last(0)
    arrive(w5[0])
    wh, wl = split(jnp.concatenate([wo[0, 0], wo[0, 1]], 0))
    cpl = dot3(xh[:256, :256], xl[:256, :256], wh, wl)
    cpl_ref[0:256] = cpl
    ch, cl = split(cpl)
    for b in range(4):
        rows = slice(b * 256, b * 256 + 256)
        p_ref[rows] = t_ref[rows] - dot3(*qa[b], ch, cl)
    w_last(1)
    lower = dot3(xh[256:, :256], xl[256:, :256], wh, wl)
    arrive(w5[1])
    wh, wl = split(jnp.concatenate([wo[1, 0], wo[1, 1]], 0))
    cpl_ref[256:512] = lower + dot3(xh[256:, 256:], xl[256:, 256:], wh, wl)
    for f in pending:
        f().wait_send()


def tail_kernel(p_ref, qh_ref, ql_ref, cpl_in, r_in, out_ref, cpl_out, r_out, ch, cl):
    i = pl.program_id(0)

    @pl.when(i == 0)
    def _():
        ch[...], cl[...] = split(cpl_in[256:512])

    rows = pl.ds(pl.multiple_of(i * 128, 128), 128)
    cpl_out[...] = cpl_in[rows]
    r_out[...] = r_in[rows]
    out_ref[...] = p_ref[...] - dot3(qh_ref[...], ql_ref[...], ch[...], cl[...])


def shards(panel_matrix, trailing):
    V = pl.BlockSpec(memory_space=pltpu.VMEM)
    ANY = pl.BlockSpec(memory_space=pl.ANY)
    f = lambda *s: jax.ShapeDtypeStruct(s, F32)
    h = lambda *s: jax.ShapeDtypeStruct(s, BF16)
    v = lambda *s: pltpu.VMEM(s, F32)
    vh = lambda *s: pltpu.VMEM(s, BF16)
    dma = pltpu.SemaphoreType.DMA
    r, part, qh, ql, cpl = pl.pallas_call(
        comm_kernel,
        out_shape=(f(512, 512), f(1024, 1024), h(4, 256, 256), h(4, 256, 256), f(512, 1024)),
        in_specs=[ANY, ANY],
        out_specs=(V,) * 5,
        scratch_shapes=[
            v(4, 256, 512), v(1024, 1024), vh(1024, 1024), vh(1024, 1024), v(512, 512), v(512, 512),
            v(2, 256, 128), v(2, 384, 128), v(256, 128), v(384, 128), v(256, 128), v(512, 128),
            v(3, 64, 128), v(64, 128), v(7, 8, 128), v(7, 64, 128), v(64, 128), v(3, 16, 128),
            v(4, 8, 128), v(4, 16, 128), v(2, 256, 128), v(2, 512, 128),
            v(2, 2, 128, 1024), v(2, 128, 1024), v(2, 2, 128, 1024),
            v(2, 3, 32, WP), v(2, 32, WP), v(2, 7, 8, 384),
            v(2, 7, 16, 1024 - WP), v(2, 16, 1024 - WP), v(2, 3, 8, 128),
            dma((150,)), dma((150,)), dma((2,)),
        ],
        name="reduce_and_factor",
        compiler_params=pltpu.CompilerParams(collective_id=0, has_side_effects=True, vmem_limit_bytes=48 * 2**20),
    )(panel_matrix, trailing)

    whole = lambda *s: pl.BlockSpec(s, lambda i: (0,) * len(s))
    rows = lambda *s: pl.BlockSpec(s, lambda i: (i, 0))
    block = pl.BlockSpec((None, 256, 256), lambda i: (i, 0, 0))
    projected, coupling, r = pl.pallas_call(
        tail_kernel,
        grid=(4,),
        out_shape=(f(1024, 1024), f(512, 1024), f(512, 512)),
        in_specs=[rows(256, 1024), block, block, whole(512, 1024), whole(512, 512)],
        out_specs=(rows(256, 1024), rows(128, 1024), rows(128, 512)),
        scratch_shapes=[vh(256, 1024), vh(256, 1024)],
        name="project",
        compiler_params=pltpu.CompilerParams(vmem_limit_bytes=24 * 2**20),
    )(part, qh, ql, cpl, r)
    return r, coupling, projected


def solution(mesh):
    in_specs = (P(("row", "col"), None), P("row", "col"))
    out_specs = (P(), P(None, "col"), P("row", "col"))
    return jax.shard_map(shards, mesh=mesh, in_specs=in_specs, out_specs=out_specs, check_vma=False)
```

```python
import jax
import jax.numpy as jnp
from jax import lax
from jax.experimental import pallas as pl
from jax.experimental.pallas import tpu as pltpu
from jax.sharding import PartitionSpec as P

HI = lax.Precision.HIGHEST
F32 = jnp.float32
BF16 = jnp.bfloat16
MESH = pl.DeviceIdType.MESH
B8 = (8, 128)

NX, NY, NZ = 4, 4, 8
BLOCKS0 = [(0, 0), (0, 1), (0, 2), (0, 3)]
BLOCKS1 = [(1, 1), (1, 2), (1, 3), (2, 2), (2, 3), (3, 3)]


def split(x):
    hi = x.astype(BF16)
    return hi, (x - hi.astype(F32)).astype(BF16)


def dot(a, b):
    return jnp.dot(a, b, preferred_element_type=F32)


def dot3(ah, al, bh, bl):
    return dot(ah, bh) + (dot(ah, bl) + dot(al, bh))


def dot_hi(a, b):
    return jnp.dot(a, b, precision=HI, preferred_element_type=F32)


def bc(v):
    return jnp.broadcast_to(v, B8)


def factor128(block, halfway=None):
    n, nb = 16, 8
    sub = lax.broadcasted_iota(jnp.int32, B8, 0)
    lan = lax.broadcasted_iota(jnp.int32, B8, 1)
    S = [block[8 * g : 8 * g + 8] for g in range(n)]
    X = [jnp.where(sub + 8 * g == lan, 1.0, 0.0).astype(F32) for g in range(n)]
    for b in range(0, n, nb):
        e = b + nb
        own = None
        for g in range(b, e):
            if own is None:
                own = [bc(S[g][:, 8 * g + c : 8 * g + c + 1]) for c in range(8)]
            C = {(c, g): own[c] for c in range(8)}
            N = None
            if g + 1 < e:
                N = [bc(S[g + 1][:, 8 * (g + 1) + c : 8 * (g + 1) + c + 1]) for c in range(8)]
            for h in range(g + 1, e):
                for c in range(8):
                    C[c, h] = bc(S[h][:, 8 * g + c : 8 * g + c + 1])
            D = jnp.zeros(B8, F32)
            for k in range(8):
                piv = bc(C[k, g][k : k + 1, :])
                rinv = 1.0 / piv
                D = jnp.where(sub == k, piv, D)
                row_s, row_x = bc(S[g][k : k + 1, :]), bc(X[g][k : k + 1, :])
                row_c = {c: bc(C[c, g][k : k + 1, :]) for c in range(k + 1, 8)}
                for h in range(g, e):
                    m = C[k, h]
                    if h == g:
                        if k == 7:
                            continue
                        m = jnp.where(sub > k, m, 0.0)
                        for c in range(k + 1, 8):
                            C[c, h] = C[c, h] - (m * row_c[c]) * rinv
                        t = m * rinv
                    else:
                        t = m * rinv
                        for c in range(k + 1, 8):
                            C[c, h] = C[c, h] - t * row_c[c]
                        if h == g + 1:
                            for c in range(8):
                                N[c] = N[c] - t * bc(m[c : c + 1, :])
                    S[h] = S[h] - t * row_s
                    X[h] = X[h] - t * row_x
            own = N
            scale = lax.rsqrt(D)
            S[g] = S[g] * scale
            X[g] = X[g] * scale
        if e < n:
            if halfway is not None:
                halfway()
            U = jnp.concatenate(S[b:e], 0)
            both = jnp.concatenate([U, jnp.concatenate(X[b:e], 0)], 1)
            up = dot_hi(U.T[8 * e :], both)
            for h in range(e, n):
                S[h] = S[h] - up[8 * (h - e) : 8 * (h - e) + 8, :128]
                X[h] = X[h] - up[8 * (h - e) : 8 * (h - e) + 8, 128:]
    R = [jnp.where(lan >= sub + 8 * g, S[g], 0.0) for g in range(n)]
    return jnp.concatenate(R, 0), jnp.concatenate(X, 0)


def comm_kernel(
    a_hbm, t_hbm,
    r_ref, p_ref, qh_ref, ql_ref, cpl_ref,
    ag, t_ref, th, tl, s_ref, x_ref, gb0, gb1, gc0, gc1, ga0, ga1,
    gl10, gr10, gl20, gl11, gr11, gl21, xb0, xb1, go0, go1,
    w_ref, wc, wo, wl1, wr1, wl2,
    send, recv, lsem,
):
    r = lax.axis_index("row")
    x = lax.axis_index("col")
    c = r % 2
    z = (r // 2) % NZ
    y = r // (2 * NZ)

    def at_y(d):
        return {"row": (((y + d) % NY) * NZ + z) * 2 + c}

    def at_z(d):
        return {"row": (y * NZ + (z + d) % NZ) * 2 + c}

    def at_x(d):
        return {"col": (x + d) % NX}

    sibling = {"row": r + 1 - 2 * c}
    axes = {"x": (NX, x, at_x), "y": (NY, y, at_y), "z": (NZ, z, at_z)}
    counter = [0]
    pending = []

    def copies(pairs, whole):
        k = counter[0]
        counter[0] += 1
        return k, pairs, whole

    def start(group):
        k, pairs, _ = group
        for src, dst, to in pairs:
            pltpu.make_async_remote_copy(
                src_ref=src, dst_ref=dst, send_sem=send.at[k], recv_sem=recv.at[k], device_id=to, device_id_type=MESH
            ).start()
        pending.append(group)

    def arrive(group):
        k, _, whole = group
        pltpu.make_async_copy(whole, whole, recv.at[k]).wait()

    def sent():
        for k, _, whole in pending:
            pltpu.make_async_copy(whole, whole, send.at[k]).wait()
        pending.clear()

    def rows_of(n):
        return lambda i: (pl.ds(pl.multiple_of(i * n, 8), n), slice(None))

    def halves_of(cols):
        return lambda i: (pl.ds(pl.multiple_of(i // 2 * 8, 8), 8), pl.ds(pl.multiple_of(i % 2 * cols, 128), cols))

    def scatter(axis, ref, piece, land):
        n, i, at = axes[axis]
        return copies([(ref.at[piece((i + d) % n)], land.at[d - 1], at(d)) for d in range(1, n)], land)

    def summed(axis, ref, piece, land):
        n, i, _ = axes[axis]
        total = ref[piece(i)]
        for d in range(n - 1):
            total = total + land[d]
        return total

    def gather(axis, ref, piece, land):
        n, i, at = axes[axis]
        return copies([(ref.at[piece(i)], ref.at[piece(i)], at(d)) for d in range(1, n)], land)

    barrier = pltpu.get_barrier_semaphore()
    peers = [sibling] + [at_y(d) for d in range(1, NY)] + [at_z(d) for d in range(1, NZ)] + [at_x(d) for d in range(1, NX)]
    for p in peers:
        pl.semaphore_signal(barrier, inc=1, device_id=p, device_id_type=MESH)
    load_a = pltpu.make_async_copy(a_hbm, ag.at[x], lsem.at[0])
    load_t = pltpu.make_async_copy(t_hbm, t_ref, lsem.at[1])
    load_a.start()
    load_t.start()
    load_a.wait()

    a_own = ag[x]
    a_own_t = a_own.T
    for i in range(4):
        rows = dot_hi(a_own_t[i * 128 : i * 128 + 128], a_own[:, i * 128 :])
        for j in range(i, 4):
            part = rows[:, (j - i) * 128 : (j - i) * 128 + 128]
            if i == 0:
                n = BLOCKS0.index((i, j))
                gb0[n // 2, n % 2 * 128 : n % 2 * 128 + 128, :] = part
            else:
                n = BLOCKS1.index((i, j))
                gb1[n // 3, n % 3 * 128 : n % 3 * 128 + 128, :] = part

    pl.semaphore_wait(barrier, len(peers))

    g0_c = copies([(gb0.at[1 - c], gc0, sibling)], gc0)
    g1_c = copies([(gb1.at[1 - c], gc1, sibling)], gc1)
    start(g0_c)
    start(g1_c)
    left, right, opposite = (x + NX - 1) % NX, (x + 1) % NX, (x + 2) % NX
    half = [slice(0, 256), slice(256, 512)]
    a1 = [
        copies([(ag.at[x, :, half[k]], ag.at[x, :, half[k]], at_x(d)) for d in (1, NX - 1)], ag.at[0])
        for k in range(2)
    ]
    a2 = [
        copies([
            (ag.at[left, 0:128, half[k]], ag.at[left, 0:128, half[k]], at_x(1)),
            (ag.at[right, 128:256, half[k]], ag.at[right, 128:256, half[k]], at_x(NX - 1)),
        ], ag.at[0, 0:128])
        for k in range(2)
    ]
    start(a1[0])
    start(a1[1])

    def w_block(b, k, first=False):
        ah, al = split(ag[b, :, half[k]].T)
        rows = pl.ds(pl.multiple_of(b * 256, 256), 256)
        for n in range(4):
            cols = slice(n * 256, n * 256 + 256)
            v = dot3(ah, al, th[rows, cols], tl[rows, cols])
            for m in range(2):
                part = v[m * 128 : m * 128 + 128]
                w_ref[k, m, :, cols] = part if first else w_ref[k, m, :, cols] + part

    s10 = scatter("z", ga0, rows_of(32), gl10)
    s20 = scatter("y", gr10, rows_of(8), gl20)
    s11 = scatter("y", ga1, rows_of(128), gl11)
    s21 = scatter("z", gr11, rows_of(16), gl21)
    x0 = copies([(xb0.at[x], xb0.at[x], at_x(d)) for d in range(1, NX)], xb0.at[0:3])
    x1 = copies([(xb1.at[x], xb1.at[x], at_x(d)) for d in range(1, NX)], xb1.at[0:3])
    o20 = gather("y", go0.at[c], lambda i: (pl.ds(pl.multiple_of(z * 32 + i * 8, 8), 8), slice(None)), gl20)
    o10 = gather("z", go0.at[c], rows_of(32), gl10)
    o21 = gather("z", go1.at[c], lambda i: (pl.ds(pl.multiple_of(y * 128 + i * 16, 8), 16), slice(None)), gl21)
    o11 = gather("y", go1.at[c], rows_of(128), gl11)
    o_c0 = copies([(go0.at[c], go0.at[c], sibling)], go0.at[c])
    o_c1 = copies([(go1.at[c, 0:384], go1.at[c, 0:384], sibling)], go1.at[c, 0:384])

    zpiece = halves_of(512)
    wk = [w_ref.at[k, c] for k in range(2)]
    ok = [wo.at[k, c] for k in range(2)]

    def in_y(i):
        return (pl.ds(pl.multiple_of(y * 32 + i // 2 * 8, 8), 8), pl.ds(pl.multiple_of(i % 2 * 512, 128), 512))

    w_c = [copies([(w_ref.at[k, 1 - c], wc.at[k], sibling)], wc.at[k]) for k in range(2)]
    w1 = [scatter("y", wk[k], rows_of(32), wl1.at[k]) for k in range(2)]
    w2 = [scatter("z", wr1.at[k], zpiece, wl2.at[k]) for k in range(2)]
    w3 = [gather("z", ok[k], in_y, wl2.at[k]) for k in range(2)]
    w4 = [gather("y", ok[k], rows_of(32), wl1.at[k]) for k in range(2)]
    w5 = [copies([(ok[k], ok[k], sibling)], ok[k]) for k in range(2)]

    def w_core(k):
        arrive(w_c[k])
        w_ref[k, c] = w_ref[k, c] + wc[k]
        start(w1[k])

    def w_first(k):
        arrive(w1[k])
        wr1[k] = summed("y", wk[k], rows_of(32), wl1.at[k])
        start(w2[k])

    def w_second(k):
        arrive(w2[k])
        ok[k][in_y(z)] = summed("z", wr1.at[k], zpiece, wl2.at[k])
        start(w3[k])

    def w_third(k):
        arrive(w3[k])
        start(w4[k])

    def w_last(k):
        arrive(w4[k])
        start(w5[k])

    arrive(g0_c)
    ga0[...] = gb0[c] + gc0[...]
    start(s10)
    arrive(g1_c)
    ga1[0:384] = gb1[c] + gc1[...]
    ga1[384:512] = jnp.zeros((128, 128), F32)
    start(s11)

    load_t.wait()
    th[...], tl[...] = split(t_ref[...])
    w_block(x, 0, True)

    arrive(s10)
    gr10[...] = summed("z", ga0, rows_of(32), gl10)
    start(s20)
    arrive(s11)
    gr11[...] = summed("y", ga1, rows_of(128), gl11)
    start(s21)
    arrive(a1[0])
    start(a2[0])
    w_block(left, 0)
    arrive(s20)
    xb0[x] = summed("y", gr10, rows_of(8), gl20)
    start(x0)
    arrive(s21)
    xb1[x] = summed("z", gr11, rows_of(16), gl21)
    start(x1)
    w_block(right, 0)
    arrive(a1[1])
    start(a2[1])
    arrive(x0)
    go0[c, pl.ds(pl.multiple_of(z * 32 + y * 8, 8), 8), :] = (xb0[0] + xb0[1]) + (xb0[2] + xb0[3])
    start(o20)
    arrive(x1)
    go1[c, pl.ds(pl.multiple_of(y * 128 + z * 16, 8), 16), :] = (xb1[0] + xb1[1]) + (xb1[2] + xb1[3])
    start(o21)
    arrive(a2[0])
    w_block(opposite, 0)
    start(w_c[0])
    w_block(x, 1, True)
    arrive(o20)
    start(o10)
    arrive(o21)
    start(o11)
    w_core(0)
    w_block(left, 1)
    w_block(right, 1)
    arrive(o10)
    start(o_c0)
    arrive(a2[1])
    w_block(opposite, 1)
    start(w_c[1])
    arrive(o_c0)
    for n, (i, j) in enumerate(BLOCKS0):
        s_ref[:128, j * 128 : j * 128 + 128] = go0[n // 2, n % 2 * 128 : n % 2 * 128 + 128, :]
    r_ref[...] = jnp.zeros_like(r_ref)
    x_ref[...] = jnp.zeros_like(x_ref)
    arrive(o11)
    start(o_c1)
    w_core(1)

    diag = s_ref[0:128, 0:128]
    for J in range(4):
        a, b, q = J * 128, J * 128 + 128, J * 128 + 256
        if J == 0:
            w_first(0)
        r11, li = factor128(diag, {1: lambda: w_first(1), 2: lambda: w_third(0)}.get(J))
        r_ref[a:b, a:b] = r11
        x_ref[a:b, a:b] = li
        if J == 0:
            arrive(o_c1)
            for n, (i, j) in enumerate(BLOCKS1):
                s_ref[i * 128 : i * 128 + 128, j * 128 : j * 128 + 128] = go1[n // 3, n % 3 * 128 : n % 3 * 128 + 128, :]
            w_second(0)
        if J == 2:
            w_second(1)
        if J < 3:
            r12 = dot_hi(li, s_ref[a:b, b:q])
            r_ref[a:b, b:q] = r12
            diag = s_ref[b:q, b:q] - dot_hi(r12.T, r12)
            if J < 2:
                r13 = dot_hi(li, s_ref[a:b, q:])
                r_ref[a:b, q:] = r13
                s_ref[b:q, q:] = s_ref[b:q, q:] - dot_hi(r12.T, r13)
                s_ref[q:, q:] = s_ref[q:, q:] - dot_hi(r13.T, r13)
        if J > 0:
            x_ref[a:b, :a] = dot_hi(li, x_ref[a:b, :a])
        if J < 3:
            x_ref[b:, :b] = x_ref[b:, :b] - dot_hi(r_ref[a:b, b:].T, x_ref[a:b, :b])

    xi = x_ref[...]
    xh, xl = split(xi)
    xth, xtl = split(xi.T)

    def basis(rows, cols):
        ah, al = split(ag[rows][:, : cols.stop])
        return split(dot3(ah, al, xth[: cols.stop, cols], xtl[: cols.stop, cols]))

    qa = [basis(b, half[0]) for b in range(4)]
    for b in range(4):
        qh_ref[b], ql_ref[b] = basis(b, half[1])
    w_third(1)
    w_last(0)
    arrive(w5[0])
    wh, wl = split(jnp.concatenate([wo[0, 0], wo[0, 1]], 0))
    cpl = dot3(xh[:256, :256], xl[:256, :256], wh, wl)
    cpl_ref[0:256] = cpl
    ch, cl = split(cpl)
    for b in range(4):
        rows = slice(b * 256, b * 256 + 256)
        p_ref[rows] = t_ref[rows] - dot3(*qa[b], ch, cl)
    w_last(1)
    lower = dot3(xh[256:, :256], xl[256:, :256], wh, wl)
    arrive(w5[1])
    wh, wl = split(jnp.concatenate([wo[1, 0], wo[1, 1]], 0))
    cpl_ref[256:512] = lower + dot3(xh[256:, 256:], xl[256:, 256:], wh, wl)
    sent()


def tail_kernel(p_ref, qh_ref, ql_ref, cpl_in, r_in, out_ref, cpl_out, r_out, ch, cl):
    i = pl.program_id(0)

    @pl.when(i == 0)
    def _():
        ch[...], cl[...] = split(cpl_in[256:512])

    rows = pl.ds(pl.multiple_of(i * 128, 128), 128)
    cpl_out[...] = cpl_in[rows]
    r_out[...] = r_in[rows]
    out_ref[...] = p_ref[...] - dot3(qh_ref[...], ql_ref[...], ch[...], cl[...])


def shards(panel_matrix, trailing):
    V = pl.BlockSpec(memory_space=pltpu.VMEM)
    HBM = pl.BlockSpec(memory_space=pltpu.HBM)
    f = lambda *s: jax.ShapeDtypeStruct(s, F32)
    h = lambda *s: jax.ShapeDtypeStruct(s, BF16)
    v = lambda *s: pltpu.VMEM(s, F32)
    vh = lambda *s: pltpu.VMEM(s, BF16)
    dma = pltpu.SemaphoreType.DMA
    r, part, qh, ql, cpl = pl.pallas_call(
        comm_kernel,
        out_shape=(f(512, 512), f(1024, 1024), h(4, 256, 256), h(4, 256, 256), f(512, 1024)),
        in_specs=[HBM, HBM],
        out_specs=(V,) * 5,
        scratch_shapes=[
            v(4, 256, 512), v(1024, 1024), vh(1024, 1024), vh(1024, 1024), v(512, 512), v(512, 512),
            v(2, 256, 128), v(2, 384, 128), v(256, 128), v(384, 128), v(256, 128), v(512, 128),
            v(7, 32, 128), v(32, 128), v(3, 8, 128), v(3, 128, 128), v(128, 128), v(7, 16, 128),
            v(4, 8, 128), v(4, 16, 128), v(2, 256, 128), v(2, 512, 128),
            v(2, 2, 128, 1024), v(2, 128, 1024), v(2, 2, 128, 1024),
            v(2, 3, 32, 1024), v(2, 32, 1024), v(2, 7, 8, 512),
            dma((40,)), dma((40,)), dma((2,)),
        ],
        name="reduce_and_factor",
        compiler_params=pltpu.CompilerParams(collective_id=0, has_side_effects=True, vmem_limit_bytes=45 * 2**20),
    )(panel_matrix, trailing)

    whole = lambda *s: pl.BlockSpec(s, lambda i: (0,) * len(s))
    rows = lambda *s: pl.BlockSpec(s, lambda i: (i, 0))
    block = pl.BlockSpec((None, 256, 256), lambda i: (i, 0, 0))
    projected, coupling, r = pl.pallas_call(
        tail_kernel,
        grid=(4,),
        out_shape=(f(1024, 1024), f(512, 1024), f(512, 512)),
        in_specs=[rows(256, 1024), block, block, whole(512, 1024), whole(512, 512)],
        out_specs=(rows(256, 1024), rows(128, 1024), rows(128, 512)),
        scratch_shapes=[vh(256, 1024), vh(256, 1024)],
        name="project",
        compiler_params=pltpu.CompilerParams(vmem_limit_bytes=24 * 2**20),
    )(part, qh, ql, cpl, r)
    return r, coupling, projected


def solution(mesh):
    in_specs = (P(("row", "col"), None), P("row", "col"))
    out_specs = (P(), P(None, "col"), P("row", "col"))
    return jax.shard_map(shards, mesh=mesh, in_specs=in_specs, out_specs=out_specs, check_vma=False)
```

```python
import jax
import jax.numpy as jnp
from jax import lax
from jax.experimental import pallas as pl
from jax.experimental.pallas import tpu as pltpu
from jax.sharding import PartitionSpec as P

HI = lax.Precision.HIGHEST
F32 = jnp.float32
BF16 = jnp.bfloat16
MESH = pl.DeviceIdType.MESH
B8 = (8, 128)

NX, NY, NZ = 4, 4, 8
BLOCKS0 = [(0, 0), (0, 1), (0, 2), (0, 3)]
BLOCKS1 = [(1, 1), (1, 2), (1, 3), (2, 2), (2, 3), (3, 3)]


def split(x):
    hi = x.astype(BF16)
    return hi, (x - hi.astype(F32)).astype(BF16)


def dot(a, b):
    return jnp.dot(a, b, preferred_element_type=F32)


def dot3(ah, al, bh, bl):
    return dot(ah, bh) + (dot(ah, bl) + dot(al, bh))


def dot_hi(a, b):
    return jnp.dot(a, b, precision=HI, preferred_element_type=F32)


def bc(v):
    return jnp.broadcast_to(v, B8)


def factor128(block, halfway=None):
    n, nb = 16, 8
    sub = lax.broadcasted_iota(jnp.int32, B8, 0)
    lan = lax.broadcasted_iota(jnp.int32, B8, 1)
    S = [block[8 * g : 8 * g + 8] for g in range(n)]
    X = [jnp.where(sub + 8 * g == lan, 1.0, 0.0).astype(F32) for g in range(n)]
    for b in range(0, n, nb):
        e = b + nb
        own = None
        for g in range(b, e):
            if own is None:
                own = [bc(S[g][:, 8 * g + c : 8 * g + c + 1]) for c in range(8)]
            C = {(c, g): own[c] for c in range(8)}
            N = None
            if g + 1 < e:
                N = [bc(S[g + 1][:, 8 * (g + 1) + c : 8 * (g + 1) + c + 1]) for c in range(8)]
            for h in range(g + 1, e):
                for c in range(8):
                    C[c, h] = bc(S[h][:, 8 * g + c : 8 * g + c + 1])
            D = jnp.zeros(B8, F32)
            for k in range(8):
                piv = bc(C[k, g][k : k + 1, :])
                rinv = 1.0 / piv
                D = jnp.where(sub == k, piv, D)
                row_s, row_x = bc(S[g][k : k + 1, :]), bc(X[g][k : k + 1, :])
                row_c = {c: bc(C[c, g][k : k + 1, :]) for c in range(k + 1, 8)}
                for h in range(g, e):
                    m = C[k, h]
                    if h == g:
                        if k == 7:
                            continue
                        m = jnp.where(sub > k, m, 0.0)
                        for c in range(k + 1, 8):
                            C[c, h] = C[c, h] - (m * row_c[c]) * rinv
                        t = m * rinv
                    else:
                        t = m * rinv
                        for c in range(k + 1, 8):
                            C[c, h] = C[c, h] - t * row_c[c]
                        if h == g + 1:
                            for c in range(8):
                                N[c] = N[c] - t * bc(m[c : c + 1, :])
                    S[h] = S[h] - t * row_s
                    X[h] = X[h] - t * row_x
            own = N
            scale = lax.rsqrt(D)
            S[g] = S[g] * scale
            X[g] = X[g] * scale
        if e < n:
            if halfway is not None:
                halfway()
            U = jnp.concatenate(S[b:e], 0)
            both = jnp.concatenate([U, jnp.concatenate(X[b:e], 0)], 1)
            up = dot_hi(U.T[8 * e :], both)
            for h in range(e, n):
                S[h] = S[h] - up[8 * (h - e) : 8 * (h - e) + 8, :128]
                X[h] = X[h] - up[8 * (h - e) : 8 * (h - e) + 8, 128:]
    R = [jnp.where(lan >= sub + 8 * g, S[g], 0.0) for g in range(n)]
    return jnp.concatenate(R, 0), jnp.concatenate(X, 0)


def comm_kernel(
    a_hbm, t_hbm,
    r_ref, p_ref, qh_ref, ql_ref, cpl_ref,
    ag, t_ref, th, tl, s_ref, x_ref, gb0, gb1, gc0, gc1, ga0, ga1,
    gl10, gr10, gl20, gl11, gr11, gl21, xb0, xb1, go0, go1,
    w_ref, wc, wo, wl1, wr1, wl2,
    send, recv, lsem,
):
    r = lax.axis_index("row")
    x = lax.axis_index("col")
    c = r % 2
    z = (r // 2) % NZ
    y = r // (2 * NZ)

    def at_y(d):
        return {"row": (((y + d) % NY) * NZ + z) * 2 + c}

    def at_z(d):
        return {"row": (y * NZ + (z + d) % NZ) * 2 + c}

    def at_x(d):
        return {"col": (x + d) % NX}

    sibling = {"row": r + 1 - 2 * c}
    axes = {"x": (NX, x, at_x), "y": (NY, y, at_y), "z": (NZ, z, at_z)}
    counter = [0]
    pending = []

    def copies(pairs, whole):
        k = counter[0]
        counter[0] += 1
        return k, pairs, whole

    def start(group):
        k, pairs, _ = group
        for src, dst, to in pairs:
            pltpu.make_async_remote_copy(
                src_ref=src, dst_ref=dst, send_sem=send.at[k], recv_sem=recv.at[k], device_id=to, device_id_type=MESH
            ).start()
        pending.append(group)

    def arrive(group):
        k, _, whole = group
        pltpu.make_async_copy(whole, whole, recv.at[k]).wait()

    def sent():
        for k, _, whole in pending:
            pltpu.make_async_copy(whole, whole, send.at[k]).wait()
        pending.clear()

    def rows_of(n):
        return lambda i: (pl.ds(pl.multiple_of(i * n, 8), n), slice(None))

    def scatter(axis, ref, piece, land):
        n, i, at = axes[axis]
        return copies([(ref.at[piece((i + d) % n)], land.at[d - 1], at(d)) for d in range(1, n)], land)

    def summed(axis, ref, piece, land):
        n, i, _ = axes[axis]
        total = ref[piece(i)]
        for d in range(n - 1):
            total = total + land[d]
        return total

    def gather(axis, ref, piece, land):
        n, i, at = axes[axis]
        return copies([(ref.at[piece(i)], ref.at[piece(i)], at(d)) for d in range(1, n)], land)

    barrier = pltpu.get_barrier_semaphore()
    peers = [sibling] + [at_y(d) for d in range(1, NY)] + [at_z(d) for d in range(1, NZ)] + [at_x(d) for d in range(1, NX)]
    for p in peers:
        pl.semaphore_signal(barrier, inc=1, device_id=p, device_id_type=MESH)
    load_a = pltpu.make_async_copy(a_hbm, ag.at[x], lsem.at[0])
    load_t = pltpu.make_async_copy(t_hbm, t_ref, lsem.at[1])
    load_a.start()
    load_t.start()
    load_a.wait()

    a_own = ag[x]
    a_own_t = a_own.T
    for i in range(4):
        rows = dot_hi(a_own_t[i * 128 : i * 128 + 128], a_own[:, i * 128 :])
        for j in range(i, 4):
            part = rows[:, (j - i) * 128 : (j - i) * 128 + 128]
            if i == 0:
                n = BLOCKS0.index((i, j))
                gb0[n // 2, n % 2 * 128 : n % 2 * 128 + 128, :] = part
            else:
                n = BLOCKS1.index((i, j))
                gb1[n // 3, n % 3 * 128 : n % 3 * 128 + 128, :] = part

    pl.semaphore_wait(barrier, len(peers))

    g0_c = copies([(gb0.at[1 - c], gc0, sibling)], gc0)
    g1_c = copies([(gb1.at[1 - c], gc1, sibling)], gc1)
    start(g0_c)
    start(g1_c)
    left, right, opposite = (x + NX - 1) % NX, (x + 1) % NX, (x + 2) % NX
    part = [slice(128 * k, 128 * k + 128) for k in range(4)]
    a1 = [
        copies([(ag.at[x, :, part[k]], ag.at[x, :, part[k]], at_x(d)) for d in (1, NX - 1)], ag.at[0, 0:128])
        for k in range(4)
    ]
    a2 = [
        copies([
            (ag.at[left, 0:128, part[k]], ag.at[left, 0:128, part[k]], at_x(1)),
            (ag.at[right, 128:256, part[k]], ag.at[right, 128:256, part[k]], at_x(NX - 1)),
        ], ag.at[0, 0:64])
        for k in range(4)
    ]
    for k in range(4):
        start(a1[k])

    def w_block(b, k, n, first=False):
        ah, al = split(ag[b, :, 128 * k : 128 * (k + n)].T)
        rows = pl.ds(pl.multiple_of(b * 256, 256), 256)
        for q in range(4):
            cols = slice(q * 256, q * 256 + 256)
            v = dot3(ah, al, th[rows, cols], tl[rows, cols])
            for m in range(2 * n):
                part_m = v[m * 64 : m * 64 + 64]
                k_m = k + m // 2
                w_ref[k_m, m % 2, :, cols] = part_m if first else w_ref[k_m, m % 2, :, cols] + part_m

    s10 = scatter("z", ga0, rows_of(32), gl10)
    s20 = scatter("y", gr10, rows_of(8), gl20)
    s11 = scatter("y", ga1, rows_of(128), gl11)
    s21 = scatter("z", gr11, rows_of(16), gl21)
    x0 = copies([(xb0.at[x], xb0.at[x], at_x(d)) for d in range(1, NX)], xb0.at[0:3])
    x1 = copies([(xb1.at[x], xb1.at[x], at_x(d)) for d in range(1, NX)], xb1.at[0:3])
    o20 = gather("y", go0.at[c], lambda i: (pl.ds(pl.multiple_of(z * 32 + i * 8, 8), 8), slice(None)), gl20)
    o10 = gather("z", go0.at[c], rows_of(32), gl10)
    o21 = gather("z", go1.at[c], lambda i: (pl.ds(pl.multiple_of(y * 128 + i * 16, 8), 16), slice(None)), gl21)
    o11 = gather("y", go1.at[c], rows_of(128), gl11)
    o_c0 = copies([(go0.at[c], go0.at[c], sibling)], go0.at[c])
    o_c1 = copies([(go1.at[c, 0:384], go1.at[c, 0:384], sibling)], go1.at[c, 0:384])

    wk = [w_ref.at[k, c] for k in range(4)]
    ok = [wo.at[k, c] for k in range(4)]

    def quarter(i, first_row=0):
        return (
            pl.ds(pl.multiple_of(first_row + i // 4 * 8, 8), 8),
            pl.ds(pl.multiple_of(i % 4 * 256, 128), 256),
        )

    def in_y(i):
        return quarter(i, y * 16)

    w_c = [copies([(w_ref.at[k, 1 - c], wc.at[k], sibling)], wc.at[k]) for k in range(4)]
    w1 = [scatter("y", wk[k], rows_of(16), wl1.at[k]) for k in range(4)]
    w2 = [scatter("z", wr1.at[k], quarter, wl2.at[k]) for k in range(4)]
    w3 = [gather("z", ok[k], in_y, wl2.at[k]) for k in range(4)]
    w4 = [gather("y", ok[k], rows_of(16), wl1.at[k]) for k in range(4)]
    w5 = [copies([(ok[k], ok[k], sibling)], ok[k]) for k in range(4)]

    def w_core(k):
        arrive(w_c[k])
        w_ref[k, c] = w_ref[k, c] + wc[k]
        start(w1[k])

    def w_first(k):
        arrive(w1[k])
        wr1[k] = summed("y", wk[k], rows_of(16), wl1.at[k])
        start(w2[k])

    def w_second(k):
        arrive(w2[k])
        ok[k][in_y(z)] = summed("z", wr1.at[k], quarter, wl2.at[k])
        start(w3[k])

    def w_third(k):
        arrive(w3[k])
        start(w4[k])

    def w_last(k):
        arrive(w4[k])
        start(w5[k])

    arrive(g0_c)
    ga0[...] = gb0[c] + gc0[...]
    start(s10)
    arrive(g1_c)
    ga1[0:384] = gb1[c] + gc1[...]
    ga1[384:512] = jnp.zeros((128, 128), F32)
    start(s11)

    load_t.wait()
    th[...], tl[...] = split(t_ref[...])
    w_block(x, 0, 4, True)

    def pass_on(k):
        arrive(a1[k])
        start(a2[k])

    def opposite_block(k):
        arrive(a2[k])
        w_block(opposite, k, 1)
        start(w_c[k])

    pass_on(0)
    arrive(s10)
    gr10[...] = summed("z", ga0, rows_of(32), gl10)
    start(s20)
    arrive(s11)
    gr11[...] = summed("y", ga1, rows_of(128), gl11)
    start(s21)
    pass_on(1)
    w_block(left, 0, 2)
    w_block(right, 0, 2)
    pass_on(2)
    arrive(s20)
    xb0[x] = summed("y", gr10, rows_of(8), gl20)
    start(x0)
    arrive(s21)
    xb1[x] = summed("z", gr11, rows_of(16), gl21)
    start(x1)
    opposite_block(0)
    pass_on(3)
    w_block(left, 2, 2)
    w_block(right, 2, 2)
    w_core(0)
    opposite_block(1)
    arrive(x0)
    go0[c, pl.ds(pl.multiple_of(z * 32 + y * 8, 8), 8), :] = (xb0[0] + xb0[1]) + (xb0[2] + xb0[3])
    start(o20)
    arrive(x1)
    go1[c, pl.ds(pl.multiple_of(y * 128 + z * 16, 8), 16), :] = (xb1[0] + xb1[1]) + (xb1[2] + xb1[3])
    start(o21)
    w_core(1)
    opposite_block(2)
    w_core(2)
    arrive(o20)
    start(o10)
    opposite_block(3)
    w_first(0)
    arrive(o21)
    start(o11)
    w_core(3)
    w_first(1)
    r_ref[...] = jnp.zeros_like(r_ref)
    x_ref[...] = jnp.zeros_like(x_ref)
    arrive(o10)
    start(o_c0)
    w_first(2)
    arrive(o_c0)
    for n, (i, j) in enumerate(BLOCKS0):
        s_ref[:128, j * 128 : j * 128 + 128] = go0[n // 2, n % 2 * 128 : n % 2 * 128 + 128, :]
    arrive(o11)
    start(o_c1)
    w_second(0)

    def at_half(J):
        if J == 0:
            w_first(3)
            w_second(1)
        if J == 1:
            w_third(0)
            w_second(3)
        if J == 2:
            w_third(2)
        if J == 3:
            w_last(1)

    def at_end(J):
        if J == 0:
            w_second(2)
        if J == 1:
            w_third(1)
        if J == 2:
            w_third(3)
            w_last(0)
        if J == 3:
            w_last(2)

    diag = s_ref[0:128, 0:128]
    for J in range(4):
        a, b, q = J * 128, J * 128 + 128, J * 128 + 256
        r11, li = factor128(diag, lambda: at_half(J))
        r_ref[a:b, a:b] = r11
        x_ref[a:b, a:b] = li
        if J == 0:
            arrive(o_c1)
            for n, (i, j) in enumerate(BLOCKS1):
                s_ref[i * 128 : i * 128 + 128, j * 128 : j * 128 + 128] = go1[n // 3, n % 3 * 128 : n % 3 * 128 + 128, :]
        at_end(J)
        if J < 3:
            r12 = dot_hi(li, s_ref[a:b, b:q])
            r_ref[a:b, b:q] = r12
            diag = s_ref[b:q, b:q] - dot_hi(r12.T, r12)
            if J < 2:
                r13 = dot_hi(li, s_ref[a:b, q:])
                r_ref[a:b, q:] = r13
                s_ref[b:q, q:] = s_ref[b:q, q:] - dot_hi(r12.T, r13)
                s_ref[q:, q:] = s_ref[q:, q:] - dot_hi(r13.T, r13)
        if J > 0:
            x_ref[a:b, :a] = dot_hi(li, x_ref[a:b, :a])
        if J < 3:
            x_ref[b:, :b] = x_ref[b:, :b] - dot_hi(r_ref[a:b, b:].T, x_ref[a:b, :b])

    xi = x_ref[...]
    xh, xl = split(xi)
    xth, xtl = split(xi.T)

    def basis(rows, cols):
        ah, al = split(ag[rows][:, : cols.stop])
        return split(dot3(ah, al, xth[: cols.stop, cols], xtl[: cols.stop, cols]))

    most, last = slice(0, 384), slice(384, 512)
    qa = [basis(b, most) for b in range(4)]
    for b in range(4):
        qh_ref[b], ql_ref[b] = basis(b, last)
    arrive(w5[0])
    arrive(w5[1])
    wh, wl = split(wo[0:2].reshape(256, 1024))
    cpl_a = dot3(xh[:256, :256], xl[:256, :256], wh, wl)
    cpl_b = dot3(xh[256:, :256], xl[256:, :256], wh, wl)
    cpl_ref[0:256] = cpl_a
    w_last(3)
    arrive(w5[2])
    wh, wl = split(wo[2].reshape(128, 1024))
    cpl_b = cpl_b + dot3(xh[256:, 256:384], xl[256:, 256:384], wh, wl)
    cpl_ref[256:384] = cpl_b[:128]
    ch, cl = split(jnp.concatenate([cpl_a, cpl_b[:128]], 0))
    for b in range(4):
        rows = slice(b * 256, b * 256 + 256)
        p_ref[rows] = t_ref[rows] - dot3(*qa[b], ch, cl)
    arrive(w5[3])
    wh, wl = split(wo[3].reshape(128, 1024))
    cpl_ref[384:512] = cpl_b[128:] + dot3(xh[384:, 384:], xl[384:, 384:], wh, wl)
    sent()


def tail_kernel(p_ref, qh_ref, ql_ref, cpl_in, r_in, out_ref, cpl_out, r_out, ch, cl):
    i = pl.program_id(0)

    @pl.when(i == 0)
    def _():
        ch[...], cl[...] = split(cpl_in[384:512])

    rows = pl.ds(pl.multiple_of(i * 128, 128), 128)
    cpl_out[...] = cpl_in[rows]
    r_out[...] = r_in[rows]
    out_ref[...] = p_ref[...] - dot3(qh_ref[...], ql_ref[...], ch[...], cl[...])


def shards(panel_matrix, trailing):
    V = pl.BlockSpec(memory_space=pltpu.VMEM)
    HBM = pl.BlockSpec(memory_space=pltpu.HBM)
    f = lambda *s: jax.ShapeDtypeStruct(s, F32)
    h = lambda *s: jax.ShapeDtypeStruct(s, BF16)
    v = lambda *s: pltpu.VMEM(s, F32)
    vh = lambda *s: pltpu.VMEM(s, BF16)
    dma = pltpu.SemaphoreType.DMA
    r, part, qh, ql, cpl = pl.pallas_call(
        comm_kernel,
        out_shape=(f(512, 512), f(1024, 1024), h(4, 256, 128), h(4, 256, 128), f(512, 1024)),
        in_specs=[HBM, HBM],
        out_specs=(V,) * 5,
        scratch_shapes=[
            v(4, 256, 512), v(1024, 1024), vh(1024, 1024), vh(1024, 1024), v(512, 512), v(512, 512),
            v(2, 256, 128), v(2, 384, 128), v(256, 128), v(384, 128), v(256, 128), v(512, 128),
            v(7, 32, 128), v(32, 128), v(3, 8, 128), v(3, 128, 128), v(128, 128), v(7, 16, 128),
            v(4, 8, 128), v(4, 16, 128), v(2, 256, 128), v(2, 512, 128),
            v(4, 2, 64, 1024), v(4, 64, 1024), v(4, 2, 64, 1024),
            v(4, 3, 16, 1024), v(4, 16, 1024), v(4, 7, 8, 256),
            dma((48,)), dma((48,)), dma((2,)),
        ],
        name="reduce_and_factor",
        compiler_params=pltpu.CompilerParams(collective_id=0, has_side_effects=True, vmem_limit_bytes=45 * 2**20),
    )(panel_matrix, trailing)

    whole = lambda *s: pl.BlockSpec(s, lambda i: (0,) * len(s))
    rows = lambda *s: pl.BlockSpec(s, lambda i: (i, 0))
    block = pl.BlockSpec((None, 256, 128), lambda i: (i, 0, 0))
    projected, coupling, r = pl.pallas_call(
        tail_kernel,
        grid=(4,),
        out_shape=(f(1024, 1024), f(512, 1024), f(512, 512)),
        in_specs=[rows(256, 1024), block, block, whole(512, 1024), whole(512, 512)],
        out_specs=(rows(256, 1024), rows(128, 1024), rows(128, 512)),
        scratch_shapes=[vh(128, 1024), vh(128, 1024)],
        name="project",
        compiler_params=pltpu.CompilerParams(vmem_limit_bytes=24 * 2**20),
    )(part, qh, ql, cpl, r)
    return r, coupling, projected


def solution(mesh):
    in_specs = (P(("row", "col"), None), P("row", "col"))
    out_specs = (P(), P(None, "col"), P("row", "col"))
    return jax.shard_map(shards, mesh=mesh, in_specs=in_specs, out_specs=out_specs, check_vma=False)
```

```python
import jax
import jax.numpy as jnp
from jax import lax
from jax.experimental import pallas as pl
from jax.experimental.pallas import tpu as pltpu
from jax.sharding import PartitionSpec as P

HI = lax.Precision.HIGHEST
F32 = jnp.float32
BF16 = jnp.bfloat16
MESH = pl.DeviceIdType.MESH
B8 = (8, 128)

NX, NY, NZ = 4, 4, 8
BLOCKS0 = [(0, 0), (0, 1), (0, 2), (0, 3)]
BLOCKS1 = [(1, 1), (1, 2), (1, 3), (2, 2), (2, 3), (3, 3)]


def split(x):
    hi = x.astype(BF16)
    return hi, (x - hi.astype(F32)).astype(BF16)


def dot(a, b):
    return jnp.dot(a, b, preferred_element_type=F32)


def dot3(ah, al, bh, bl):
    return dot(ah, bh) + (dot(ah, bl) + dot(al, bh))


def dot_hi(a, b):
    return jnp.dot(a, b, precision=HI, preferred_element_type=F32)


def bc(v):
    return jnp.broadcast_to(v, B8)


def factor128(block, halfway=None):
    n, nb = 16, 8
    sub = lax.broadcasted_iota(jnp.int32, B8, 0)
    lan = lax.broadcasted_iota(jnp.int32, B8, 1)
    S = [block[8 * g : 8 * g + 8] for g in range(n)]
    X = [jnp.where(sub + 8 * g == lan, 1.0, 0.0).astype(F32) for g in range(n)]
    for b in range(0, n, nb):
        e = b + nb
        own = None
        for g in range(b, e):
            if own is None:
                own = [bc(S[g][:, 8 * g + c : 8 * g + c + 1]) for c in range(8)]
            C = {(c, g): own[c] for c in range(8)}
            N = None
            if g + 1 < e:
                N = [bc(S[g + 1][:, 8 * (g + 1) + c : 8 * (g + 1) + c + 1]) for c in range(8)]
            for h in range(g + 1, e):
                for c in range(8):
                    C[c, h] = bc(S[h][:, 8 * g + c : 8 * g + c + 1])
            D = jnp.zeros(B8, F32)
            for k in range(8):
                piv = bc(C[k, g][k : k + 1, :])
                rinv = 1.0 / piv
                D = jnp.where(sub == k, piv, D)
                row_s, row_x = bc(S[g][k : k + 1, :]), bc(X[g][k : k + 1, :])
                row_c = {c: bc(C[c, g][k : k + 1, :]) for c in range(k + 1, 8)}
                for h in range(g, e):
                    m = C[k, h]
                    if h == g:
                        if k == 7:
                            continue
                        m = jnp.where(sub > k, m, 0.0)
                        for c in range(k + 1, 8):
                            C[c, h] = C[c, h] - (m * row_c[c]) * rinv
                        t = m * rinv
                    else:
                        t = m * rinv
                        for c in range(k + 1, 8):
                            C[c, h] = C[c, h] - t * row_c[c]
                        if h == g + 1:
                            for c in range(8):
                                N[c] = N[c] - t * bc(m[c : c + 1, :])
                    S[h] = S[h] - t * row_s
                    X[h] = X[h] - t * row_x
            own = N
            scale = lax.rsqrt(D)
            S[g] = S[g] * scale
            X[g] = X[g] * scale
        if e < n:
            if halfway is not None:
                halfway()
            U = jnp.concatenate(S[b:e], 0)
            both = jnp.concatenate([U, jnp.concatenate(X[b:e], 0)], 1)
            up = dot_hi(U.T[8 * e :], both)
            for h in range(e, n):
                S[h] = S[h] - up[8 * (h - e) : 8 * (h - e) + 8, :128]
                X[h] = X[h] - up[8 * (h - e) : 8 * (h - e) + 8, 128:]
    R = [jnp.where(lan >= sub + 8 * g, S[g], 0.0) for g in range(n)]
    return jnp.concatenate(R, 0), jnp.concatenate(X, 0)


def comm_kernel(
    a_hbm, t_hbm,
    r_ref, p_ref, qh_ref, ql_ref, cpl_ref,
    ag, t_ref, th, tl, s_ref, x_ref, gb0, gb1, gc0, gc1, ga0, ga1,
    gl10, gr10, gl20, gl11, gr11, gl21, xb0, xb1, go0, go1,
    w_ref, wc, wo, wl1, wr1, wl2,
    send, recv, lsem,
):
    r = lax.axis_index("row")
    x = lax.axis_index("col")
    c = r % 2
    z = (r // 2) % NZ
    y = r // (2 * NZ)

    def at_y(d):
        return {"row": (((y + d) % NY) * NZ + z) * 2 + c}

    def at_z(d):
        return {"row": (y * NZ + (z + d) % NZ) * 2 + c}

    def at_x(d):
        return {"col": (x + d) % NX}

    sibling = {"row": r + 1 - 2 * c}
    axes = {"x": (NX, x, at_x), "y": (NY, y, at_y), "z": (NZ, z, at_z)}
    counter = [0]
    pending = []

    def copies(pairs, whole):
        k = counter[0]
        counter[0] += 1
        return k, pairs, whole

    def start(group):
        k, pairs, _ = group
        for src, dst, to in pairs:
            pltpu.make_async_remote_copy(
                src_ref=src, dst_ref=dst, send_sem=send.at[k], recv_sem=recv.at[k], device_id=to, device_id_type=MESH
            ).start()
        pending.append(group)

    def arrive(group):
        k, _, whole = group
        pltpu.make_async_copy(whole, whole, recv.at[k]).wait()

    def sent():
        for k, _, whole in pending:
            pltpu.make_async_copy(whole, whole, send.at[k]).wait()
        pending.clear()

    def rows_of(n):
        return lambda i: (pl.ds(pl.multiple_of(i * n, 8), n), slice(None))

    def scatter(axis, ref, piece, land):
        n, i, at = axes[axis]
        return copies([(ref.at[piece((i + d) % n)], land.at[d - 1], at(d)) for d in range(1, n)], land)

    def summed(axis, ref, piece, land):
        n, i, _ = axes[axis]
        total = ref[piece(i)]
        for d in range(n - 1):
            total = total + land[d]
        return total

    def gather(axis, ref, piece, land):
        n, i, at = axes[axis]
        return copies([(ref.at[piece(i)], ref.at[piece(i)], at(d)) for d in range(1, n)], land)

    barrier = pltpu.get_barrier_semaphore()
    peers = [sibling] + [at_y(d) for d in range(1, NY)] + [at_z(d) for d in range(1, NZ)] + [at_x(d) for d in range(1, NX)]
    for p in peers:
        pl.semaphore_signal(barrier, inc=1, device_id=p, device_id_type=MESH)
    load_a = pltpu.make_async_copy(a_hbm, ag.at[x], lsem.at[0])
    load_t = pltpu.make_async_copy(t_hbm, t_ref, lsem.at[1])
    load_a.start()
    load_t.start()
    load_a.wait()

    pl.semaphore_wait(barrier, len(peers))

    left, right, opposite = (x + NX - 1) % NX, (x + 1) % NX, (x + 2) % NX
    part = [slice(128 * k, 128 * k + 128) for k in range(4)]
    a1 = [
        copies([(ag.at[x, :, part[k]], ag.at[x, :, part[k]], at_x(d)) for d in (1, NX - 1)], ag.at[0, 0:128])
        for k in range(4)
    ]
    a2 = [
        copies([
            (ag.at[left, 0:128, part[k]], ag.at[left, 0:128, part[k]], at_x(1)),
            (ag.at[right, 128:256, part[k]], ag.at[right, 128:256, part[k]], at_x(NX - 1)),
        ], ag.at[0, 0:64])
        for k in range(4)
    ]
    for k in range(4):
        start(a1[k])

    a_own = ag[x]
    a_own_t = a_own.T
    for i in range(4):
        rows = dot_hi(a_own_t[i * 128 : i * 128 + 128], a_own[:, i * 128 :])
        for j in range(i, 4):
            part = rows[:, (j - i) * 128 : (j - i) * 128 + 128]
            if i == 0:
                n = BLOCKS0.index((i, j))
                gb0[n // 2, n % 2 * 128 : n % 2 * 128 + 128, :] = part
            else:
                n = BLOCKS1.index((i, j))
                gb1[n // 3, n % 3 * 128 : n % 3 * 128 + 128, :] = part

    g0_c = copies([(gb0.at[1 - c], gc0, sibling)], gc0)
    g1_c = copies([(gb1.at[1 - c], gc1, sibling)], gc1)
    start(g0_c)
    start(g1_c)

    def w_block(b, k, n, first=False):
        ah, al = split(ag[b, :, 128 * k : 128 * (k + n)].T)
        rows = pl.ds(pl.multiple_of(b * 256, 256), 256)
        for q in range(4):
            cols = slice(q * 256, q * 256 + 256)
            v = dot3(ah, al, th[rows, cols], tl[rows, cols])
            for m in range(2 * n):
                part_m = v[m * 64 : m * 64 + 64]
                k_m = k + m // 2
                w_ref[k_m, m % 2, :, cols] = part_m if first else w_ref[k_m, m % 2, :, cols] + part_m

    s10 = scatter("z", ga0, rows_of(32), gl10)
    s20 = scatter("y", gr10, rows_of(8), gl20)
    s11 = scatter("y", ga1, rows_of(128), gl11)
    s21 = scatter("z", gr11, rows_of(16), gl21)
    x0 = copies([(xb0.at[x], xb0.at[x], at_x(d)) for d in range(1, NX)], xb0.at[0:3])
    x1 = copies([(xb1.at[x], xb1.at[x], at_x(d)) for d in range(1, NX)], xb1.at[0:3])
    o20 = gather("y", go0.at[c], lambda i: (pl.ds(pl.multiple_of(z * 32 + i * 8, 8), 8), slice(None)), gl20)
    o10 = gather("z", go0.at[c], rows_of(32), gl10)
    o21 = gather("z", go1.at[c], lambda i: (pl.ds(pl.multiple_of(y * 128 + i * 16, 8), 16), slice(None)), gl21)
    o11 = gather("y", go1.at[c], rows_of(128), gl11)
    o_c0 = copies([(go0.at[c], go0.at[c], sibling)], go0.at[c])
    o_c1 = copies([(go1.at[c, 0:384], go1.at[c, 0:384], sibling)], go1.at[c, 0:384])

    wk = [w_ref.at[k, c] for k in range(4)]
    ok = [wo.at[k, c] for k in range(4)]

    def quarter(i, first_row=0):
        return (
            pl.ds(pl.multiple_of(first_row + i // 4 * 8, 8), 8),
            pl.ds(pl.multiple_of(i % 4 * 256, 128), 256),
        )

    def in_y(i):
        return quarter(i, y * 16)

    w_c = [copies([(w_ref.at[k, 1 - c], wc.at[k], sibling)], wc.at[k]) for k in range(4)]
    w1 = [scatter("y", wk[k], rows_of(16), wl1.at[k]) for k in range(4)]
    w2 = [scatter("z", wr1.at[k], quarter, wl2.at[k]) for k in range(4)]
    w3 = [gather("z", ok[k], in_y, wl2.at[k]) for k in range(4)]
    w4 = [gather("y", ok[k], rows_of(16), wl1.at[k]) for k in range(4)]
    w5 = [copies([(ok[k], ok[k], sibling)], ok[k]) for k in range(4)]

    def w_core(k):
        arrive(w_c[k])
        w_ref[k, c] = w_ref[k, c] + wc[k]
        start(w1[k])

    def w_first(k):
        arrive(w1[k])
        wr1[k] = summed("y", wk[k], rows_of(16), wl1.at[k])
        start(w2[k])

    def w_second(k):
        arrive(w2[k])
        ok[k][in_y(z)] = summed("z", wr1.at[k], quarter, wl2.at[k])
        start(w3[k])

    def w_third(k):
        arrive(w3[k])
        start(w4[k])

    def w_last(k):
        arrive(w4[k])
        start(w5[k])

    def pass_on(k):
        arrive(a1[k])
        start(a2[k])

    def opposite_block(k):
        arrive(a2[k])
        w_block(opposite, k, 1)
        start(w_c[k])

    arrive(g0_c)
    ga0[...] = gb0[c] + gc0[...]
    start(s10)
    arrive(g1_c)
    ga1[0:384] = gb1[c] + gc1[...]
    ga1[384:512] = jnp.zeros((128, 128), F32)
    start(s11)
    load_t.wait()
    th[...], tl[...] = split(t_ref[...])
    w_block(x, 0, 4, True)
    pass_on(0)
    arrive(s10)
    gr10[...] = summed("z", ga0, rows_of(32), gl10)
    start(s20)
    arrive(s11)
    gr11[...] = summed("y", ga1, rows_of(128), gl11)
    start(s21)
    pass_on(1)
    w_block(left, 0, 2)
    w_block(right, 0, 2)
    pass_on(2)
    arrive(s20)
    xb0[x] = summed("y", gr10, rows_of(8), gl20)
    start(x0)
    arrive(s21)
    xb1[x] = summed("z", gr11, rows_of(16), gl21)
    start(x1)
    opposite_block(0)
    pass_on(3)
    opposite_block(1)
    w_core(0)
    w_block(left, 2, 2)
    w_block(right, 2, 2)
    arrive(x0)
    go0[c, pl.ds(pl.multiple_of(z * 32 + y * 8, 8), 8), :] = (xb0[0] + xb0[1]) + (xb0[2] + xb0[3])
    start(o20)
    arrive(x1)
    go1[c, pl.ds(pl.multiple_of(y * 128 + z * 16, 8), 16), :] = (xb1[0] + xb1[1]) + (xb1[2] + xb1[3])
    start(o21)
    w_core(1)
    opposite_block(2)
    opposite_block(3)
    w_core(2)
    w_first(0)
    w_core(3)
    arrive(o20)
    start(o10)
    arrive(o21)
    start(o11)
    w_first(1)
    r_ref[...] = jnp.zeros_like(r_ref)
    x_ref[...] = jnp.zeros_like(x_ref)
    w_first(2)
    arrive(o10)
    start(o_c0)
    arrive(o11)
    start(o_c1)
    w_second(0)
    w_first(3)
    arrive(o_c0)
    for n, (i, j) in enumerate(BLOCKS0):
        s_ref[:128, j * 128 : j * 128 + 128] = go0[n // 2, n % 2 * 128 : n % 2 * 128 + 128, :]

    def at_half(J):
        if J == 0:
            w_second(1)
        if J == 1:
            w_third(0)
            w_second(3)
        if J == 2:
            w_third(2)
        if J == 3:
            w_last(1)

    def at_end(J):
        if J == 0:
            w_second(2)
        if J == 1:
            w_third(1)
        if J == 2:
            w_third(3)
            w_last(0)

    diag = s_ref[0:128, 0:128]
    for J in range(4):
        a, b, q = J * 128, J * 128 + 128, J * 128 + 256
        r11, li = factor128(diag, lambda: at_half(J))
        r_ref[a:b, a:b] = r11
        x_ref[a:b, a:b] = li
        if J == 0:
            arrive(o_c1)
            for n, (i, j) in enumerate(BLOCKS1):
                s_ref[i * 128 : i * 128 + 128, j * 128 : j * 128 + 128] = go1[n // 3, n % 3 * 128 : n % 3 * 128 + 128, :]
        at_end(J)
        if J < 3:
            r12 = dot_hi(li, s_ref[a:b, b:q])
            r_ref[a:b, b:q] = r12
            diag = s_ref[b:q, b:q] - dot_hi(r12.T, r12)
            if J < 2:
                r13 = dot_hi(li, s_ref[a:b, q:])
                r_ref[a:b, q:] = r13
                s_ref[b:q, q:] = s_ref[b:q, q:] - dot_hi(r12.T, r13)
                s_ref[q:, q:] = s_ref[q:, q:] - dot_hi(r13.T, r13)
        if J > 0:
            x_ref[a:b, :a] = dot_hi(li, x_ref[a:b, :a])
        if J < 3:
            x_ref[b:, :b] = x_ref[b:, :b] - dot_hi(r_ref[a:b, b:].T, x_ref[a:b, :b])

    xi = x_ref[...]
    xh, xl = split(xi)
    xth, xtl = split(xi.T)

    def basis(rows, cols):
        ah, al = split(ag[rows][:, : cols.stop])
        return split(dot3(ah, al, xth[: cols.stop, cols], xtl[: cols.stop, cols]))

    most, last = slice(0, 384), slice(384, 512)
    qa = [basis(b, most) for b in range(4)]
    for b in range(4):
        qh_ref[b], ql_ref[b] = basis(b, last)
    w_last(2)
    arrive(w5[0])
    arrive(w5[1])
    wh, wl = split(wo[0:2].reshape(256, 1024))
    cpl_a = dot3(xh[:256, :256], xl[:256, :256], wh, wl)
    cpl_b = dot3(xh[256:, :256], xl[256:, :256], wh, wl)
    cpl_ref[0:256] = cpl_a
    w_last(3)
    arrive(w5[2])
    wh, wl = split(wo[2].reshape(128, 1024))
    cpl_b = cpl_b + dot3(xh[256:, 256:384], xl[256:, 256:384], wh, wl)
    cpl_ref[256:384] = cpl_b[:128]
    ch, cl = split(jnp.concatenate([cpl_a, cpl_b[:128]], 0))
    for b in range(4):
        rows = slice(b * 256, b * 256 + 256)
        p_ref[rows] = t_ref[rows] - dot3(*qa[b], ch, cl)
    arrive(w5[3])
    wh, wl = split(wo[3].reshape(128, 1024))
    cpl_ref[384:512] = cpl_b[128:] + dot3(xh[384:, 384:], xl[384:, 384:], wh, wl)
    sent()


def tail_kernel(p_ref, qh_ref, ql_ref, cpl_in, r_in, out_ref, cpl_out, r_out, ch, cl):
    i = pl.program_id(0)

    @pl.when(i == 0)
    def _():
        ch[...], cl[...] = split(cpl_in[384:512])

    rows = pl.ds(pl.multiple_of(i * 128, 128), 128)
    cpl_out[...] = cpl_in[rows]
    r_out[...] = r_in[rows]
    block = pl.ds(pl.multiple_of(i * 256, 256), 256)
    out_ref[...] = p_ref[block] - dot3(qh_ref[i], ql_ref[i], ch[...], cl[...])


def shards(panel_matrix, trailing):
    V = pl.BlockSpec(memory_space=pltpu.VMEM)
    HBM = pl.BlockSpec(memory_space=pltpu.HBM)
    f = lambda *s: jax.ShapeDtypeStruct(s, F32)
    h = lambda *s: jax.ShapeDtypeStruct(s, BF16)
    v = lambda *s: pltpu.VMEM(s, F32)
    vh = lambda *s: pltpu.VMEM(s, BF16)
    dma = pltpu.SemaphoreType.DMA
    r, part, qh, ql, cpl = pl.pallas_call(
        comm_kernel,
        out_shape=(f(512, 512), f(1024, 1024), h(4, 256, 128), h(4, 256, 128), f(512, 1024)),
        in_specs=[HBM, HBM],
        out_specs=(V,) * 5,
        scratch_shapes=[
            v(4, 256, 512), v(1024, 1024), vh(1024, 1024), vh(1024, 1024), v(512, 512), v(512, 512),
            v(2, 256, 128), v(2, 384, 128), v(256, 128), v(384, 128), v(256, 128), v(512, 128),
            v(7, 32, 128), v(32, 128), v(3, 8, 128), v(3, 128, 128), v(128, 128), v(7, 16, 128),
            v(4, 8, 128), v(4, 16, 128), v(2, 256, 128), v(2, 512, 128),
            v(4, 2, 64, 1024), v(4, 64, 1024), v(4, 2, 64, 1024),
            v(4, 3, 16, 1024), v(4, 16, 1024), v(4, 7, 8, 256),
            dma((48,)), dma((48,)), dma((2,)),
        ],
        name="reduce_and_factor",
        compiler_params=pltpu.CompilerParams(collective_id=0, has_side_effects=True, vmem_limit_bytes=45 * 2**20),
    )(panel_matrix, trailing)

    rows = lambda *s: pl.BlockSpec(s, lambda i: (i, 0))
    projected, coupling, r = pl.pallas_call(
        tail_kernel,
        grid=(4,),
        out_shape=(f(1024, 1024), f(512, 1024), f(512, 512)),
        in_specs=[V] * 5,
        out_specs=(rows(256, 1024), rows(128, 1024), rows(128, 512)),
        scratch_shapes=[vh(128, 1024), vh(128, 1024)],
        name="project",
        compiler_params=pltpu.CompilerParams(vmem_limit_bytes=24 * 2**20),
    )(part, qh, ql, cpl, r)
    return r, coupling, projected


def solution(mesh):
    in_specs = (P(("row", "col"), None), P("row", "col"))
    out_specs = (P(), P(None, "col"), P("row", "col"))
    return jax.shard_map(shards, mesh=mesh, in_specs=in_specs, out_specs=out_specs, check_vma=False)
```

```python
import jax
import jax.numpy as jnp
from jax import lax
from jax.experimental import pallas as pl
from jax.experimental.pallas import tpu as pltpu
from jax.sharding import PartitionSpec as P

HI = lax.Precision.HIGHEST
F32 = jnp.float32
BF16 = jnp.bfloat16
MESH = pl.DeviceIdType.MESH
B8 = (8, 128)

NX, NY, NZ = 4, 4, 8
BLOCKS0 = [(0, 0), (0, 1), (0, 2), (0, 3)]
BLOCKS1 = [(1, 1), (1, 2), (1, 3), (2, 2), (2, 3), (3, 3)]


def split(x):
    hi = x.astype(BF16)
    return hi, (x - hi.astype(F32)).astype(BF16)


def dot(a, b):
    return jnp.dot(a, b, preferred_element_type=F32)


def dot3(ah, al, bh, bl):
    return dot(ah, bh) + (dot(ah, bl) + dot(al, bh))


def dot_hi(a, b):
    return jnp.dot(a, b, precision=HI, preferred_element_type=F32)


def bc(v):
    return jnp.broadcast_to(v, B8)


def factor128(block, halfway=None):
    n, nb = 16, 8
    sub = lax.broadcasted_iota(jnp.int32, B8, 0)
    lan = lax.broadcasted_iota(jnp.int32, B8, 1)
    S = [block[8 * g : 8 * g + 8] for g in range(n)]
    X = [jnp.where(sub + 8 * g == lan, 1.0, 0.0).astype(F32) for g in range(n)]
    for b in range(0, n, nb):
        e = b + nb
        own = None
        for g in range(b, e):
            if own is None:
                own = [bc(S[g][:, 8 * g + c : 8 * g + c + 1]) for c in range(8)]
            C = {(c, g): own[c] for c in range(8)}
            N = None
            if g + 1 < e:
                N = [bc(S[g + 1][:, 8 * (g + 1) + c : 8 * (g + 1) + c + 1]) for c in range(8)]
            for h in range(g + 1, e):
                for c in range(8):
                    C[c, h] = bc(S[h][:, 8 * g + c : 8 * g + c + 1])
            D = jnp.zeros(B8, F32)
            for k in range(8):
                piv = bc(C[k, g][k : k + 1, :])
                rinv = 1.0 / piv
                D = jnp.where(sub == k, piv, D)
                row_s, row_x = bc(S[g][k : k + 1, :]), bc(X[g][k : k + 1, :])
                row_c = {c: bc(C[c, g][k : k + 1, :]) for c in range(k + 1, 8)}
                for h in range(g, e):
                    m = C[k, h]
                    if h == g:
                        if k == 7:
                            continue
                        m = jnp.where(sub > k, m, 0.0)
                        for c in range(k + 1, 8):
                            C[c, h] = C[c, h] - (m * row_c[c]) * rinv
                        t = m * rinv
                    else:
                        t = m * rinv
                        for c in range(k + 1, 8):
                            C[c, h] = C[c, h] - t * row_c[c]
                        if h == g + 1:
                            for c in range(8):
                                N[c] = N[c] - t * bc(m[c : c + 1, :])
                    S[h] = S[h] - t * row_s
                    X[h] = X[h] - t * row_x
            own = N
            scale = lax.rsqrt(D)
            S[g] = S[g] * scale
            X[g] = X[g] * scale
        if e < n:
            if halfway is not None:
                halfway()
            U = jnp.concatenate(S[b:e], 0)
            both = jnp.concatenate([U, jnp.concatenate(X[b:e], 0)], 1)
            up = dot_hi(U.T[8 * e :], both)
            for h in range(e, n):
                S[h] = S[h] - up[8 * (h - e) : 8 * (h - e) + 8, :128]
                X[h] = X[h] - up[8 * (h - e) : 8 * (h - e) + 8, 128:]
    R = [jnp.where(lan >= sub + 8 * g, S[g], 0.0) for g in range(n)]
    return jnp.concatenate(R, 0), jnp.concatenate(X, 0)


def comm_kernel(
    a_hbm, t_hbm,
    r_ref, p_ref, qh_ref, ql_ref, cpl_ref,
    ag, t_ref, th, tl, s_ref, x_ref, gb0, gb1, gc0, gc1, ga0, ga1,
    gl10, gr10, gl20, gl11, gr11, gl21, xb0, xb1, go0, go1,
    w_ref, wc, wo, wl1, wr1, wl2,
    send, recv, lsem,
):
    r = lax.axis_index("row")
    x = lax.axis_index("col")
    c = r % 2
    z = (r // 2) % NZ
    y = r // (2 * NZ)

    def at_y(d):
        return {"row": (((y + d) % NY) * NZ + z) * 2 + c}

    def at_z(d):
        return {"row": (y * NZ + (z + d) % NZ) * 2 + c}

    def at_x(d):
        return {"col": (x + d) % NX}

    sibling = {"row": r + 1 - 2 * c}
    axes = {"x": (NX, x, at_x), "y": (NY, y, at_y), "z": (NZ, z, at_z)}
    counter = [0]
    pending = []

    def copies(pairs, whole):
        k = counter[0]
        counter[0] += 1
        return k, pairs, whole

    def start(group):
        k, pairs, _ = group
        for src, dst, to in pairs:
            pltpu.make_async_remote_copy(
                src_ref=src, dst_ref=dst, send_sem=send.at[k], recv_sem=recv.at[k], device_id=to, device_id_type=MESH
            ).start()
        pending.append(group)

    def arrive(group):
        k, _, whole = group
        pltpu.make_async_copy(whole, whole, recv.at[k]).wait()

    def sent(but=0):
        done = pending[: len(pending) - but]
        for k, _, whole in done:
            pltpu.make_async_copy(whole, whole, send.at[k]).wait()
        del pending[: len(done)]

    def rows_of(n):
        return lambda i: (pl.ds(pl.multiple_of(i * n, 8), n), slice(None))

    def scatter(axis, ref, piece, land):
        n, i, at = axes[axis]
        return copies([(ref.at[piece((i + d) % n)], land.at[d - 1], at(d)) for d in range(1, n)], land)

    def summed(axis, ref, piece, land):
        n, i, _ = axes[axis]
        total = ref[piece(i)]
        for d in range(n - 1):
            total = total + land[d]
        return total

    def gather(axis, ref, piece, land):
        n, i, at = axes[axis]
        return copies([(ref.at[piece(i)], ref.at[piece(i)], at(d)) for d in range(1, n)], land)

    barrier = pltpu.get_barrier_semaphore()
    peers = [sibling] + [at_y(d) for d in range(1, NY)] + [at_z(d) for d in range(1, NZ)] + [at_x(d) for d in range(1, NX)]
    for p in peers:
        pl.semaphore_signal(barrier, inc=1, device_id=p, device_id_type=MESH)
    load_a = pltpu.make_async_copy(a_hbm, ag.at[x], lsem.at[0])
    load_t = pltpu.make_async_copy(t_hbm, t_ref, lsem.at[1])
    load_a.start()
    load_t.start()
    load_a.wait()

    a_own = ag[x]
    a_own_t = a_own.T
    for i in range(4):
        rows = dot_hi(a_own_t[i * 128 : i * 128 + 128], a_own[:, i * 128 :])
        for j in range(i, 4):
            part = rows[:, (j - i) * 128 : (j - i) * 128 + 128]
            if i == 0:
                n = BLOCKS0.index((i, j))
                gb0[n // 2, n % 2 * 128 : n % 2 * 128 + 128, :] = part
            else:
                n = BLOCKS1.index((i, j))
                gb1[n // 3, n % 3 * 128 : n % 3 * 128 + 128, :] = part

    pl.semaphore_wait(barrier, len(peers))

    g0_c = copies([(gb0.at[1 - c], gc0, sibling)], gc0)
    g1_c = copies([(gb1.at[1 - c], gc1, sibling)], gc1)
    start(g0_c)
    start(g1_c)
    left, right, opposite = (x + NX - 1) % NX, (x + 1) % NX, (x + 2) % NX
    part = [slice(128 * k, 128 * k + 128) for k in range(4)]
    a1 = [
        copies([(ag.at[x, :, part[k]], ag.at[x, :, part[k]], at_x(d)) for d in (1, NX - 1)], ag.at[0, 0:128])
        for k in range(4)
    ]
    a2 = [
        copies([
            (ag.at[left, 0:128, part[k]], ag.at[left, 0:128, part[k]], at_x(1)),
            (ag.at[right, 128:256, part[k]], ag.at[right, 128:256, part[k]], at_x(NX - 1)),
        ], ag.at[0, 0:64])
        for k in range(4)
    ]
    for k in range(4):
        start(a1[k])

    def w_block(b, k, n, first=False):
        ah, al = split(ag[b, :, 128 * k : 128 * (k + n)].T)
        rows = pl.ds(pl.multiple_of(b * 256, 256), 256)
        for q in range(4):
            cols = slice(q * 256, q * 256 + 256)
            v = dot3(ah, al, th[rows, cols], tl[rows, cols])
            for m in range(2 * n):
                part_m = v[m * 64 : m * 64 + 64]
                k_m = k + m // 2
                w_ref[k_m, m % 2, :, cols] = part_m if first else w_ref[k_m, m % 2, :, cols] + part_m

    s10 = scatter("z", ga0, rows_of(32), gl10)
    s20 = scatter("y", gr10, rows_of(8), gl20)
    s11 = scatter("y", ga1, rows_of(128), gl11)
    s21 = scatter("z", gr11, rows_of(16), gl21)
    x0 = copies([(xb0.at[x], xb0.at[x], at_x(d)) for d in range(1, NX)], xb0.at[0:3])
    x1 = copies([(xb1.at[x], xb1.at[x], at_x(d)) for d in range(1, NX)], xb1.at[0:3])
    o20 = gather("y", go0.at[c], lambda i: (pl.ds(pl.multiple_of(z * 32 + i * 8, 8), 8), slice(None)), gl20)
    o10 = gather("z", go0.at[c], rows_of(32), gl10)
    o21 = gather("z", go1.at[c], lambda i: (pl.ds(pl.multiple_of(y * 128 + i * 16, 8), 16), slice(None)), gl21)
    o11 = gather("y", go1.at[c], rows_of(128), gl11)
    o_c0 = copies([(go0.at[c], go0.at[c], sibling)], go0.at[c])
    o_c1 = copies([(go1.at[c, 0:384], go1.at[c, 0:384], sibling)], go1.at[c, 0:384])

    wk = [w_ref.at[k, c] for k in range(4)]
    ok = [wo.at[k, c] for k in range(4)]

    def quarter(i, first_row=0):
        return (
            pl.ds(pl.multiple_of(first_row + i // 4 * 8, 8), 8),
            pl.ds(pl.multiple_of(i % 4 * 256, 128), 256),
        )

    def in_y(i):
        return quarter(i, y * 16)

    w_c = [copies([(w_ref.at[k, 1 - c], wc.at[k], sibling)], wc.at[k]) for k in range(4)]
    w1 = [scatter("y", wk[k], rows_of(16), wl1.at[k]) for k in range(4)]
    w2 = [scatter("z", wr1.at[k], quarter, wl2.at[k]) for k in range(4)]
    w3 = [gather("z", ok[k], in_y, wl2.at[k]) for k in range(4)]
    w4 = [gather("y", ok[k], rows_of(16), wl1.at[k]) for k in range(4)]
    w5 = [copies([(ok[k], ok[k], sibling)], ok[k]) for k in range(4)]

    def w_core(k):
        arrive(w_c[k])
        w_ref[k, c] = w_ref[k, c] + wc[k]
        start(w1[k])

    def w_first(k):
        arrive(w1[k])
        wr1[k] = summed("y", wk[k], rows_of(16), wl1.at[k])
        start(w2[k])

    def w_second(k):
        arrive(w2[k])
        ok[k][in_y(z)] = summed("z", wr1.at[k], quarter, wl2.at[k])
        start(w3[k])

    def w_third(k):
        arrive(w3[k])
        start(w4[k])

    def w_last(k):
        arrive(w4[k])
        start(w5[k])

    arrive(g0_c)
    ga0[...] = gb0[c] + gc0[...]
    start(s10)
    arrive(g1_c)
    ga1[0:384] = gb1[c] + gc1[...]
    ga1[384:512] = jnp.zeros((128, 128), F32)
    start(s11)

    load_t.wait()
    th[...], tl[...] = split(t_ref[...])
    w_block(x, 0, 4, True)

    def pass_on(k):
        arrive(a1[k])
        start(a2[k])

    def opposite_block(k):
        arrive(a2[k])
        w_block(opposite, k, 1)
        start(w_c[k])

    pass_on(0)
    arrive(s10)
    gr10[...] = summed("z", ga0, rows_of(32), gl10)
    start(s20)
    arrive(s11)
    gr11[...] = summed("y", ga1, rows_of(128), gl11)
    start(s21)
    pass_on(1)
    w_block(left, 0, 2)
    w_block(right, 0, 2)
    pass_on(2)
    arrive(s20)
    xb0[x] = summed("y", gr10, rows_of(8), gl20)
    start(x0)
    arrive(s21)
    xb1[x] = summed("z", gr11, rows_of(16), gl21)
    start(x1)
    opposite_block(0)
    pass_on(3)
    w_block(left, 2, 2)
    w_block(right, 2, 2)
    w_core(0)
    opposite_block(1)
    arrive(x0)
    go0[c, pl.ds(pl.multiple_of(z * 32 + y * 8, 8), 8), :] = (xb0[0] + xb0[1]) + (xb0[2] + xb0[3])
    start(o20)
    arrive(x1)
    go1[c, pl.ds(pl.multiple_of(y * 128 + z * 16, 8), 16), :] = (xb1[0] + xb1[1]) + (xb1[2] + xb1[3])
    start(o21)
    w_core(1)
    opposite_block(2)
    w_core(2)
    arrive(o20)
    start(o10)
    opposite_block(3)
    w_first(0)
    arrive(o21)
    start(o11)
    w_core(3)
    w_first(1)
    r_ref[...] = jnp.zeros_like(r_ref)
    x_ref[...] = jnp.zeros_like(x_ref)
    arrive(o10)
    start(o_c0)
    w_first(2)
    arrive(o_c0)
    for n, (i, j) in enumerate(BLOCKS0):
        s_ref[:128, j * 128 : j * 128 + 128] = go0[n // 2, n % 2 * 128 : n % 2 * 128 + 128, :]
    arrive(o11)
    start(o_c1)
    w_second(0)

    def at_half(J):
        if J == 0:
            w_first(3)
            w_second(1)
        if J == 1:
            w_third(0)
            w_second(3)
        if J == 2:
            w_third(2)
        if J == 3:
            w_last(1)
            sent(8)

    def at_end(J):
        if J == 0:
            w_second(2)
        if J == 1:
            w_third(1)
        if J == 2:
            w_third(3)
            w_last(0)
        if J == 3:
            w_last(2)

    diag = s_ref[0:128, 0:128]
    for J in range(4):
        a, b, q = J * 128, J * 128 + 128, J * 128 + 256
        r11, li = factor128(diag, lambda: at_half(J))
        r_ref[a:b, a:b] = r11
        x_ref[a:b, a:b] = li
        if J == 0:
            arrive(o_c1)
            for n, (i, j) in enumerate(BLOCKS1):
                s_ref[i * 128 : i * 128 + 128, j * 128 : j * 128 + 128] = go1[n // 3, n % 3 * 128 : n % 3 * 128 + 128, :]
        at_end(J)
        if J < 3:
            r12 = dot_hi(li, s_ref[a:b, b:q])
            r_ref[a:b, b:q] = r12
            diag = s_ref[b:q, b:q] - dot_hi(r12.T, r12)
            if J < 2:
                r13 = dot_hi(li, s_ref[a:b, q:])
                r_ref[a:b, q:] = r13
                s_ref[b:q, q:] = s_ref[b:q, q:] - dot_hi(r12.T, r13)
                s_ref[q:, q:] = s_ref[q:, q:] - dot_hi(r13.T, r13)
        if J > 0:
            x_ref[a:b, :a] = dot_hi(li, x_ref[a:b, :a])
        if J < 3:
            x_ref[b:, :b] = x_ref[b:, :b] - dot_hi(r_ref[a:b, b:].T, x_ref[a:b, :b])

    xi = x_ref[...]
    xh, xl = split(xi)
    xth, xtl = split(xi.T)

    def basis(rows, cols):
        ah, al = split(ag[rows][:, : cols.stop])
        return split(dot3(ah, al, xth[: cols.stop, cols], xtl[: cols.stop, cols]))

    first, second = slice(0, 256), slice(256, 512)
    qa = [basis(b, first) for b in range(4)]
    for b in range(4):
        qh_ref[b], ql_ref[b] = basis(b, second)
    arrive(w5[0])
    arrive(w5[1])
    wh, wl = split(wo[0:2].reshape(256, 1024))
    cpl_a = dot3(xh[:256, :256], xl[:256, :256], wh, wl)
    cpl_ref[0:256] = cpl_a
    w_last(3)
    cpl_b = dot3(xh[256:, :256], xl[256:, :256], wh, wl)
    ch, cl = split(cpl_a)
    for b in range(4):
        rows = slice(b * 256, b * 256 + 256)
        p_ref[rows] = t_ref[rows] - dot3(*qa[b], ch, cl)
    arrive(w5[2])
    arrive(w5[3])
    wh, wl = split(wo[2:4].reshape(256, 1024))
    cpl_ref[256:512] = cpl_b + dot3(xh[256:, 256:], xl[256:, 256:], wh, wl)
    sent()


def tail_kernel(p_ref, qh_ref, ql_ref, cpl_in, r_in, out_ref, cpl_out, r_out, ch, cl):
    i = pl.program_id(0)

    @pl.when(i == 0)
    def _():
        ch[...], cl[...] = split(cpl_in[256:512])

    rows = pl.ds(pl.multiple_of(i * 128, 128), 128)
    cpl_out[...] = cpl_in[rows]
    r_out[...] = r_in[rows]
    block = pl.ds(pl.multiple_of(i * 256, 256), 256)
    out_ref[...] = p_ref[block] - dot3(qh_ref[i], ql_ref[i], ch[...], cl[...])


def shards(panel_matrix, trailing):
    V = pl.BlockSpec(memory_space=pltpu.VMEM)
    HBM = pl.BlockSpec(memory_space=pltpu.HBM)
    f = lambda *s: jax.ShapeDtypeStruct(s, F32)
    h = lambda *s: jax.ShapeDtypeStruct(s, BF16)
    v = lambda *s: pltpu.VMEM(s, F32)
    vh = lambda *s: pltpu.VMEM(s, BF16)
    dma = pltpu.SemaphoreType.DMA
    r, part, qh, ql, cpl = pl.pallas_call(
        comm_kernel,
        out_shape=(f(512, 512), f(1024, 1024), h(4, 256, 256), h(4, 256, 256), f(512, 1024)),
        in_specs=[HBM, HBM],
        out_specs=(V,) * 5,
        scratch_shapes=[
            v(4, 256, 512), v(1024, 1024), vh(1024, 1024), vh(1024, 1024), v(512, 512), v(512, 512),
            v(2, 256, 128), v(2, 384, 128), v(256, 128), v(384, 128), v(256, 128), v(512, 128),
            v(7, 32, 128), v(32, 128), v(3, 8, 128), v(3, 128, 128), v(128, 128), v(7, 16, 128),
            v(4, 8, 128), v(4, 16, 128), v(2, 256, 128), v(2, 512, 128),
            v(4, 2, 64, 1024), v(4, 64, 1024), v(4, 2, 64, 1024),
            v(4, 3, 16, 1024), v(4, 16, 1024), v(4, 7, 8, 256),
            dma((48,)), dma((48,)), dma((2,)),
        ],
        name="reduce_and_factor",
        compiler_params=pltpu.CompilerParams(collective_id=0, has_side_effects=True, vmem_limit_bytes=45 * 2**20),
    )(panel_matrix, trailing)

    rows = lambda *s: pl.BlockSpec(s, lambda i: (i, 0))
    projected, coupling, r = pl.pallas_call(
        tail_kernel,
        grid=(4,),
        out_shape=(f(1024, 1024), f(512, 1024), f(512, 512)),
        in_specs=[V] * 5,
        out_specs=(rows(256, 1024), rows(128, 1024), rows(128, 512)),
        scratch_shapes=[vh(256, 1024), vh(256, 1024)],
        name="project",
        compiler_params=pltpu.CompilerParams(vmem_limit_bytes=24 * 2**20),
    )(part, qh, ql, cpl, r)
    return r, coupling, projected


def solution(mesh):
    in_specs = (P(("row", "col"), None), P("row", "col"))
    out_specs = (P(), P(None, "col"), P("row", "col"))
    return jax.shard_map(shards, mesh=mesh, in_specs=in_specs, out_specs=out_specs, check_vma=False)
```
